256 devices in a mesh: dp: 32 (over z_hi, x, core), tensor: 8 (over z_lo, y).
Axes of the slice: x: 4, y: 4, z: 8 (z_hi: 4, z_lo: 2; z = z_hi * 2 + z_lo), core: 2. Of those that a mesh axis runs over, the one named last changes fastest.
Arguments:
- tokens: bfloat16 [4096, 4096], P('dp', 'tensor'), may hold values from -6 to 6
- gate_pre: bfloat16 [4096, 14336], P('dp', 'tensor'), may hold values from -12 to 12
- up_act: bfloat16 [4096, 14336], P('dp', 'tensor'), may hold values from -6 to 6
- hidden_cot: bfloat16 [4096, 14336], P('dp', 'tensor'), may hold values from -6 to 6
- source_ids: int32 [4096], P('dp'), may hold values from 0 to 63
- data_weight: float32 [64], replicated, may hold values from 0.25 to 4
- grad: float32 [4096, 14336], P('dp', 'tensor'), may hold values from -6 to 6
- moment_m: float32 [4096, 14336], P('dp', 'tensor'), may hold values from -0.0006 to 0.0006
- moment_v: float32 [4096, 14336], P('dp', 'tensor'), may hold values from 1e-09 to 1e-07
- val_adjoint: float32 [4096, 14336], P('dp', 'tensor'), may hold values from -17000 to 17000
Outputs:
- curvature: float32 [4096, 14336], P('dp', 'tensor')
- source_grad: float32 [64], replicated
The draws below stay inside these ranges and needn't reach their ends.
All inputs are finite; a program needn't handle non-finite values.
Results may differ from the reference program's by a relative error of at most 0.029.
Values may be sent and summed in bfloat16 or wider, within the bound.
A program may use at most 128 MiB of HBM per device.

```python
import math
import jax
import jax.numpy as jnp
import numpy as np
from jax import lax

D = 4096
FF = 14336
NSRC = 64
TOK_DEV = 128
TOKENS = 4096
N_DP = 32


def shared_base(key):
    return jnp.clip(jax.random.normal(key, (D, FF), jnp.float32), -6.0, 6.0)


def band_gains(key):
    row_key, col_key = jax.random.split(key)
    row_band = jnp.exp(jax.random.uniform(row_key, (32,), jnp.float32, -1.5, 1.5))
    col_band = jnp.exp(jax.random.uniform(col_key, (8,), jnp.float32, -1.5, 1.5))
    row_index = jnp.arange(D, dtype=jnp.int32) * 32 // D
    col_index = jnp.arange(FF, dtype=jnp.int32) * 8 // FF
    return (row_band[row_index][:, None], col_band[col_index][None, :])


def draw_grad(key, part):
    common = shared_base(key)
    key = jax.random.fold_in(key, 11)
    row_scale, col_scale = band_gains(jax.random.fold_in(key, 13))
    return 0.015 * row_scale * col_scale * common


def draw_val_adjoint(key, part):
    common = shared_base(key)
    key = jax.random.fold_in(key, 12)
    own_noise = jnp.clip(jax.random.normal(key, (D, FF), jnp.float32), -6.0, 6.0)
    return 2000.0 * (0.8 * common + 0.6 * own_noise)


def set_ends(array, key, low, top_value):
    dims = array.shape
    place = [jax.random.randint(jax.random.fold_in(key, axis), (), 0, dims[axis]) for axis in range(len(dims))]
    array = array.at[tuple(place)].set(low)
    longest = dims.index(max(dims))
    place[longest] = (place[longest] + 1) % dims[longest]
    return array.at[tuple(place)].set(top_value)


def block_scale(stream_key, dims, cuts, low, top_value):
    loudness, own = 1.0, jax.random.fold_in(stream_key, 6)
    for axis_at, blocks in cuts:
        heights = jnp.exp(jax.random.uniform(jax.random.fold_in(own, axis_at), (blocks,), jnp.float32, low / len(cuts), top_value / len(cuts)))
        loudness = loudness * jnp.repeat(heights, dims[axis_at] // blocks).reshape([-1 if axis == axis_at else 1 for axis in range(len(dims))])
    return loudness


def rank_table(count, skew):
    weights = [(1 << 20) // math.isqrt(rank ** skew) + 1 for rank in range(1, count + 1)]
    width = 1 + sum(weights) // (1 << 30)
    return np.cumsum(np.array([max(1, weight // width) for weight in weights]))


def ranked(key, dims, number_of, skew):
    listing = rank_table(number_of, skew)
    pick = jax.random.randint(jax.random.fold_in(key, 1), dims, 0, int(listing[number_of - 1]))
    grade = jnp.searchsorted(jnp.asarray(listing, jnp.int32), pick, side="right")
    return jax.random.permutation(jax.random.fold_in(key, 2), number_of)[grade].astype(jnp.int32)


def noise(stream_key, shape, deviation, most, shards=(), held_as=jnp.bfloat16):
    entries = deviation * jax.random.normal(stream_key, shape, jnp.float32)
    if shards:
        entries = entries * block_scale(stream_key, shape, shards, -0.22, 0.18)
    return jnp.clip(entries, -most, most).astype(held_as)


def setup_inputs(seed: int = 0) -> dict:
    key_list = jax.random.split(jax.random.key(seed), 11)
    tokens = noise(key_list[0], (TOKENS, D), 1.0, 6.0, ((0, 32), (1, 8)))
    gate_pre = noise(key_list[1], (TOKENS, FF), 2.0, 12.0, ((0, 32), (1, 8)))
    up_act = noise(key_list[2], (TOKENS, FF), 1.0, 6.0, ((0, 32), (1, 8)))
    hidden_cot = noise(key_list[3], (TOKENS, FF), 1.0, 6.0, ((0, 32), (1, 8)))
    source_ids = set_ends(ranked(key_list[4], (TOKENS,), NSRC, 1), jax.random.fold_in(key_list[4], 3), 0, NSRC - 1).astype(jnp.int32)
    data_weight = jnp.clip(jnp.exp(jax.random.uniform(key_list[5], (NSRC,), jnp.float32, math.log(0.25), math.log(4.0))), 0.25, 4.0)
    grad = draw_grad(jax.random.fold_in(key_list[10], 71), 0)
    moment_m = noise(key_list[7], (D, FF), 0.0001, 0.0006, ((0, 32), (1, 8)), jnp.float32)
    moment_v = jnp.clip(jnp.exp(math.log(1.0000000116860974e-07) - 4.6051702 * jax.random.uniform(key_list[8], (D, FF), jnp.float32) ** block_scale(key_list[8], (D, FF), ((0, 32), (1, 8)), -0.2, 0.2)), 9.999999717180685e-10, 1.0000000116860974e-07)
    val_adjoint = draw_val_adjoint(jax.random.fold_in(key_list[10], 71), 0)
    return dict(tokens=tokens, gate_pre=gate_pre, up_act=up_act, hidden_cot=hidden_cot, source_ids=source_ids, data_weight=data_weight, grad=grad, moment_m=moment_m, moment_v=moment_v, val_adjoint=val_adjoint)


CLIP_NORM = 1.0
LEARN_RATE = 0.00015
BETA_ONE = 0.9
BETA_TWO = 0.95
ADAM_EPSILON = 1e-08
NORM_EPSILON = 1e-06

def clip_terms(total_sq):
    scaled = CLIP_NORM * lax.rsqrt(total_sq)
    return jnp.minimum(scaled, 1.0)

def pulled_back(grad, moment_m, moment_v, val_adjoint, clip_factor):
    clipped = clip_factor * grad
    moment_new = BETA_ONE * moment_m + (1.0 - BETA_ONE) * clipped
    second_new = BETA_TWO * moment_v + (1.0 - BETA_TWO) * clipped * clipped
    root_v = jnp.sqrt(second_new)
    denominator = root_v + ADAM_EPSILON
    jacobian = -LEARN_RATE * ((1.0 - BETA_ONE) / denominator - moment_new * (1.0 - BETA_TWO) * clipped / (denominator * denominator * root_v))
    return jacobian * val_adjoint

def activation_terms(gate_pre, up_act, hidden_cot):
    pre_act = gate_pre.astype(jnp.float32)
    sigma = jax.nn.sigmoid(pre_act)
    first_slope = sigma * (1.0 + pre_act * (1.0 - sigma))
    second_slope = sigma * (1.0 - sigma) * (2.0 + pre_act * (1.0 - 2.0 * sigma))
    coupling = up_act.astype(jnp.float32) * hidden_cot.astype(jnp.float32)
    return (coupling * first_slope, coupling * second_slope)

def reference(tokens, gate_pre, up_act, hidden_cot, source_ids, data_weight, grad, moment_m, moment_v, val_adjoint):
    total_sq = jnp.sum(grad * grad) + NORM_EPSILON
    clip_factor = clip_terms(total_sq)
    pulled = pulled_back(grad, moment_m, moment_v, val_adjoint, clip_factor)
    tangent = (clip_factor * pulled).astype(jnp.bfloat16)
    projected = jnp.dot(tokens, tangent, preferred_element_type=jnp.float32)
    first_order, second_order = activation_terms(gate_pre, up_act, hidden_cot)
    onehot = (source_ids[:, None] == jnp.arange(NSRC, dtype=jnp.int32)[None, :]).astype(jnp.float32)
    per_tok = lax.optimization_barrier(jnp.sum(projected * first_order, axis=1))
    source_grad = lax.optimization_barrier(jnp.sum(onehot * per_tok[:, None], axis=0)) / TOKENS
    weight_tok = lax.optimization_barrier(jnp.sum(onehot * data_weight[None, :], axis=1)) / TOKENS
    mixed = (weight_tok[:, None] * second_order * projected).astype(jnp.bfloat16)
    tok_blocks = tokens.reshape(N_DP, TOK_DEV, D)
    mix_blocks = mixed.reshape(N_DP, TOK_DEV, FF)

    def add_block(running, block_pair):
        token_block, mixed_block = block_pair
        product = jnp.dot(token_block.T, mixed_block, preferred_element_type=jnp.float32)
        rounded = lax.optimization_barrier(product.astype(jnp.bfloat16))
        return (running + rounded.astype(jnp.float32), None)
    curvature, _unused = lax.scan(add_block, jnp.zeros((D, FF), jnp.float32), (tok_blocks, mix_blocks))
    return (curvature, source_grad)
```

```python
import jax
import jax.numpy as jnp
from jax import lax
from jax.experimental import pallas as pl
from jax.experimental.pallas import tpu as pltpu
from jax.sharding import PartitionSpec as P

CLIP_NORM = 1.0
LEARN_RATE = 0.00015
BETA_ONE = 0.9
BETA_TWO = 0.95
ADAM_EPSILON = 1e-08
NORM_EPSILON = 1e-06

MESH = pl.DeviceIdType.MESH
BF16 = jnp.bfloat16
F32 = jnp.float32

ROWS = 128
COLS = 1792
PART = 448
TOK = 512
TOKENS = 4096
NSRC = 64


class Slots:
    def __init__(self):
        self.used = 0

    def take(self, count):
        first = self.used
        self.used += count
        return first


SLOTS = Slots()
TZ = SLOTS.take(7)
TY = SLOTS.take(24)
XZ = SLOTS.take(4)
XX = SLOTS.take(12)
XC = SLOTS.take(16)
AZ = SLOTS.take(4)
IZ = SLOTS.take(4)
N1 = SLOTS.take(24)
CC = SLOTS.take(16)
RX = SLOTS.take(12)
RZ = SLOTS.take(4)
N2 = SLOTS.take(24)
N_SEMS = SLOTS.used


def kernel(
    tokens, gate, up, hid, ids, weight, grad, mom, sec, adj,
    out, src_out,
    grad_v, mom_v, sec_v, adj_v, gate_v, up_v, hid_v,
    tok, tang, xb, acts, act, idb, norm1, norm2, proj, mixed, cb, cr, s0, s1, s2, r0, r1, r2, fin, res,
    ls, ss, rs,
):
    dp, tn = lax.axis_index("dp"), lax.axis_index("tensor")
    zh, x, c = lax.div(dp, 8), lax.rem(lax.div(dp, 2), 4), lax.rem(dp, 2)
    zl, y = lax.div(tn, 4), lax.rem(tn, 4)
    z = zh * 2 + zl
    way = 1 - 2 * c

    def dev(z_at, x_at, y_at, c_at):
        return (lax.div(z_at, 2) * 8 + x_at * 2 + c_at, lax.rem(z_at, 2) * 4 + y_at)

    def zs(k):
        return lax.rem(z + k * way + 8, 8)

    def xs(k):
        return lax.rem(x + k * way + 4, 4)

    def ys(k):
        return lax.rem(y + k * way + 4, 4)

    def zhs(k):
        return lax.rem(zh + k + 4, 4)

    def at_zh(zh_at):
        return (zh_at * 8 + x * 2 + c, tn)

    x_dev = {k: dev(z, xs(k), y, c) for k in (1, -1)}
    y_dev = {k: dev(z, x, ys(k), c) for k in (1, -1)}
    z_dev = {k: dev(zs(k), x, y, c) for k in (1, -1)}
    core = dev(z, x, y, 1 - c)

    groups = (
        [(d, dev(z, lax.div(lax.rem(x * 2 + c + d, 8), 2), y, lax.rem(c + d, 2))) for d in range(1, 8)],
        [(d, dev(z, x, lax.rem(y + d, 4), c)) for d in range(1, 4)],
        [(d, dev(lax.rem(z + d, 8), x, y, c)) for d in range(1, 8)],
    )
    places = ((x * 2 + c, 8), (y, 4), (z, 8))

    sent = []

    def push(src, dst, sem, to):
        copy = pltpu.make_async_remote_copy(
            src_ref=src, dst_ref=dst, send_sem=ss.at[sem], recv_sem=rs.at[sem], device_id=to, device_id_type=MESH
        )
        copy.start()
        sent.append(copy)

    def arrived(dst, sem):
        pltpu.make_async_remote_copy(
            src_ref=dst, dst_ref=dst, send_sem=ss.at[sem], recv_sem=rs.at[sem], device_id=core, device_id_type=MESH
        ).wait_recv()

    local = []

    def fetch(src, dst):
        copy = pltpu.make_async_copy(src, dst, ls.at[len(local)])
        copy.start()
        local.append(copy)
        return copy

    def shard(z_at, y_at):
        block = lax.rem(z_at, 2) * 4 + y_at
        return tok.at[pl.ds(2 * block, 2), pl.ds(pl.multiple_of(lax.div(z_at, 2) * ROWS, ROWS), ROWS), :]

    def spread(buf, sems, stage, value):
        place, size = places[stage]
        buf[stage, place] = value
        for d, to in groups[stage]:
            push(buf.at[stage, place], buf.at[stage, place], sems + stage * 8 + d, to)

    def collect(buf, sems, stage):
        place, size = places[stage]
        for d in range(1, size):
            arrived(buf.at[stage, lax.rem(place + size - d, size)], sems + stage * 8 + d)
        total = buf[stage, 0]
        for k in range(1, size):
            total = total + buf[stage, k]
        return total

    get_grad = fetch(grad, grad_v)
    block = zl * 4 + y
    own_rows = pl.ds(pl.multiple_of(zh * ROWS, ROWS), ROWS)
    get_tok = [
        fetch(tokens.at[:, pl.ds(h * 256, 256)], tok.at[2 * block + h, own_rows, :]) for h in range(2)
    ]
    get_acts = [fetch(gate, gate_v), fetch(up, up_v), fetch(hid, hid_v)]
    get_rest = [fetch(mom, mom_v), fetch(sec, sec_v), fetch(adj, adj_v)]

    barrier = pltpu.get_barrier_semaphore()
    n_partners = 0
    for group in groups:
        for _, to in group:
            pl.semaphore_signal(barrier, inc=1, device_id=to, device_id_type=MESH)
            n_partners += 1
    pl.semaphore_wait(barrier, n_partners)

    get_grad.wait()

    def square(k, total):
        part = grad_v[pl.ds(pl.multiple_of(k * 8, 8), 8), :]
        part = part * part
        for j in range(COLS // 128):
            total = total + part[:, j * 128 : (j + 1) * 128]
        return total

    spread(norm1, N1, 0, lax.fori_loop(0, ROWS // 8, square, jnp.zeros((8, 128), F32)))

    for copy in get_tok:
        copy.wait()

    def pass_y(m, z_at):
        here = shard(z_at, y)
        push(here, here, TY + m, y_dev[1])
        push(here, here, TY + 8 + m, y_dev[-1])

    def relay_y(m, z_at):
        there = shard(z_at, ys(-1))
        arrived(there, TY + m)
        push(there, there, TY + 16 + m, y_dev[1])

    own = shard(z, y)
    push(own, own, TZ, z_dev[1])
    push(own, own, TZ + 4, z_dev[-1])
    pass_y(0, z)

    for copy in get_acts:
        copy.wait()
    ids_row = ids[...]
    weight_row = jnp.zeros((1, ROWS), F32)
    for k in range(NSRC):
        weight_row = jnp.where(ids_row == k, weight[k], weight_row)
    weight_row = weight_row / TOKENS
    idb[zh] = jnp.broadcast_to(ids_row.astype(F32), (8, ROWS))

    def activation(j, carry):
        cols = pl.ds(pl.multiple_of(j * 128, 128), 128)
        pre = gate_v[:, cols].astype(F32)
        sigma = 1.0 / (1.0 + jnp.exp(-pre))
        coupling = up_v[:, cols].astype(F32) * hid_v[:, cols].astype(F32)
        first = coupling * sigma * (1.0 + pre * (1.0 - sigma))
        second = coupling * sigma * (1.0 - sigma) * (2.0 + pre * (1.0 - 2.0 * sigma))
        acts[0, cols, :] = first.T.astype(BF16)
        acts[1, cols, :] = (second.T * weight_row).astype(BF16)
        return carry

    lax.fori_loop(0, COLS // 128, activation, 0)

    spread(norm1, N1, 1, collect(norm1, N1, 0))

    def forward_z(k):
        z_at = zs(-k)
        arrived(shard(z_at, y), TZ + k - 1)
        if k < 4:
            push(shard(z_at, y), shard(z_at, y), TZ + k, z_dev[1])
        pass_y(2 * k - 1, z_at)

    def backward_z(k):
        z_at = zs(k)
        arrived(shard(z_at, y), TZ + 4 + k - 1)
        if k < 3:
            push(shard(z_at, y), shard(z_at, y), TZ + 4 + k, z_dev[-1])
        pass_y(2 * k, z_at)

    forward_z(1)
    backward_z(1)
    spread(norm1, N1, 2, collect(norm1, N1, 1))
    relay_y(0, z)
    forward_z(2)
    backward_z(2)

    total_sq = jnp.sum(collect(norm1, N1, 2), keepdims=True) + NORM_EPSILON
    clip = jnp.minimum(CLIP_NORM * lax.rsqrt(total_sq), 1.0)
    for copy in get_rest:
        copy.wait()

    def tangent(j, carry):
        cols = pl.ds(pl.multiple_of(j * 128, 128), 128)
        clipped = clip * grad_v[:, cols]
        moment_new = BETA_ONE * mom_v[:, cols] + (1.0 - BETA_ONE) * clipped
        second_new = BETA_TWO * sec_v[:, cols] + (1.0 - BETA_TWO) * clipped * clipped
        root_v = jnp.sqrt(second_new)
        inverse = 1.0 / (root_v + ADAM_EPSILON)
        jacobian = -LEARN_RATE * (
            (1.0 - BETA_ONE) * inverse - moment_new * (1.0 - BETA_TWO) * clipped * (inverse * inverse / root_v)
        )
        pulled = jacobian * adj_v[:, cols]
        tang[cols, :] = (clip * pulled).T.astype(BF16)
        return carry

    lax.fori_loop(0, COLS // 128, tangent, 0)

    def part_rows(q):
        return pl.ds(pl.multiple_of(q * PART, 64), PART)

    keep = fetch(tang.at[part_rows(zh), :], xb.at[dp])
    for d in (2, 1, 3):
        push(tang.at[part_rows(zhs(d)), :], xb.at[dp], XZ + d, at_zh(zhs(d)))

    relay_y(1, zs(-1))
    relay_y(2, zs(1))
    forward_z(3)
    backward_z(3)
    relay_y(3, zs(-2))
    relay_y(4, zs(2))
    forward_z(4)

    def x_block(x_at, d):
        return xb.at[zhs(-d) * 8 + x_at * 2 + c]

    def to_core(x_at, offset, d):
        push(x_block(x_at, d), x_block(x_at, d), XC + offset * 4 + d, core)

    keep.wait()
    for d in (0, 1, 3, 2):
        here = x_block(x, d)
        if d:
            arrived(here, XZ + d)
        push(here, here, XX + d, x_dev[1])
        push(here, here, XX + 4 + d, x_dev[-1])
        to_core(x, 0, d)

    for d in (1, 3, 2):
        to = at_zh(zhs(d))
        push(acts.at[:, part_rows(zhs(d)), :], act.at[zh], AZ + d, to)
        push(idb.at[zh], idb.at[zh], IZ + d, to)
    keep_act = fetch(acts.at[:, part_rows(zh), :], act.at[zh])

    behind, ahead = 3 - 2 * c, 1 + 2 * c
    relay_y(5, zs(-3))
    relay_y(6, zs(3))
    for d in (0, 1, 3, 2):
        there = x_block(xs(-1), d)
        arrived(there, XX + d)
        push(there, there, XX + 8 + d, x_dev[1])
        to_core(xs(-1), behind, d)
        there = x_block(xs(1), d)
        arrived(there, XX + 4 + d)
        to_core(xs(1), ahead, d)
    relay_y(7, zs(-4))
    for d in (0, 1, 3, 2):
        there = x_block(xs(2), d)
        arrived(there, XX + 8 + d)
        to_core(xs(2), 2, d)

    offsets = [z] + [zs(k) for k in (-1, 1, -2, 2, -3, 3, -4)]
    for m, z_at in enumerate(offsets):
        arrived(shard(z_at, ys(1)), TY + 8 + m)
    for m, z_at in enumerate(offsets):
        arrived(shard(z_at, ys(2)), TY + 16 + m)
    for offset in range(4):
        for d in range(4):
            arrived(xb.at[zhs(-d) * 8 + lax.rem(x + offset, 4) * 2 + 1 - c], XC + offset * 4 + d)

    proj[...] = jnp.zeros_like(proj)

    def first_product(k, carry):
        left = jnp.concatenate([xb[8 * k + i] for i in range(8)], axis=1)
        right = jnp.concatenate([tok[4 * k + i] for i in range(4)], axis=1)
        proj[...] += lax.dot_general(left, right, (((1,), (1,)), ((), ())), preferred_element_type=F32)
        return carry

    lax.fori_loop(0, 4, first_product, 0)

    keep_act.wait()
    for d in (1, 3, 2):
        arrived(act.at[zhs(-d)], AZ + d)
        arrived(idb.at[zhs(-d)], IZ + d)

    sums = jnp.zeros((8, 128), F32)
    source = lax.broadcasted_iota(jnp.int32, (128, ROWS), 0).astype(F32)
    for k in range(4):
        cols = pl.ds(k * ROWS, ROWS)
        part = proj[:, cols]
        mixed[:, cols] = (part * act[k, 1].astype(F32)).astype(BF16)
        per_tok = jnp.sum(part * act[k, 0].astype(F32), axis=0, keepdims=True)
        onehot = (source == idb[k, 0:1, :]).astype(F32)
        sums = sums + lax.dot_general(
            jnp.broadcast_to(per_tok, (8, ROWS)),
            onehot,
            (((1,), (1,)), ((), ())),
            precision=lax.Precision.HIGHEST,
            preferred_element_type=F32,
        )
    order = (2, 1, 3, 0)

    def second_product(x_at, zh_at):
        whole = jnp.dot(mixed[...], tok[zh_at * 4 + x_at], preferred_element_type=F32)
        cb[x_at, zh_at, 0] = whole[:, :128].astype(BF16)
        cb[x_at, zh_at, 1] = whole[:, 128:].astype(BF16)

    def products(j):
        zh_at = zhs(order[j])
        for offset in (2, behind, ahead, 0):
            x_at = lax.rem(x + offset, 4)
            second_product(x_at, zh_at)
            push(cb.at[x_at, zh_at, 1 - c], cr.at[x_at, zh_at], CC + offset * 4 + j, core)

    def both(offset, j):
        x_at, zh_at = lax.rem(x + offset, 4), zhs(order[j])
        arrived(cr.at[x_at, zh_at], CC + offset * 4 + j)
        return cb[x_at, zh_at, c].astype(F32) + cr[x_at, zh_at].astype(F32)

    def outward(j):
        s0[j] = both(2, j).astype(BF16)
        push(s0.at[j], r0.at[j], RX + j, x_dev[1])
        s2[j] = both(behind, j).astype(BF16)
        push(s2.at[j], r2.at[j], RX + 8 + j, x_dev[-1])

    def onward(j):
        part = both(ahead, j)
        arrived(r0.at[j], RX + j)
        s1[j] = (part + r0[j].astype(F32)).astype(BF16)
        push(s1.at[j], r1.at[j], RX + 4 + j, x_dev[1])

    def finish(j):
        part = both(0, j)
        arrived(r2.at[j], RX + 8 + j)
        part = part + r2[j].astype(F32)
        arrived(r1.at[j], RX + 4 + j)
        fin[j] = (part + r1[j].astype(F32)).astype(BF16)
        d = order[j]
        if d:
            push(fin.at[j], res.at[part_rows(zh), :], RZ + d, at_zh(zhs(d)))
        else:
            res[part_rows(zh), :] = fin[j]

    products(0)
    products(1)
    outward(0)
    products(2)
    outward(1)
    products(3)
    outward(2)
    outward(3)
    spread(norm2, N2, 0, sums)
    onward(0)
    onward(1)
    spread(norm2, N2, 1, collect(norm2, N2, 0))
    onward(2)
    onward(3)
    finish(0)
    spread(norm2, N2, 2, collect(norm2, N2, 1))
    finish(1)
    finish(2)
    finish(3)
    src_out[...] = collect(norm2, N2, 2) / TOKENS
    for d in (1, 3, 2):
        arrived(res.at[part_rows(zhs(-d)), :], RZ + d)

    def emit(j, carry):
        cols = pl.ds(pl.multiple_of(j * 128, 128), 128)
        out[:, cols] = res[cols, :].astype(F32).T
        return carry

    lax.fori_loop(0, COLS // 128, emit, 0)
    for copy in sent:
        copy.wait_send()


def body(tokens, gate_pre, up_act, hidden_cot, source_ids, data_weight, grad, moment_m, moment_v, val_adjoint):
    hbm = pl.BlockSpec(memory_space=pl.ANY)
    vmem = pl.BlockSpec(memory_space=pltpu.VMEM)
    smem = pl.BlockSpec(memory_space=pltpu.SMEM)
    curvature, sums = pl.pallas_call(
        kernel,
        name="metagradient",
        out_shape=(jax.ShapeDtypeStruct((ROWS, COLS), F32), jax.ShapeDtypeStruct((8, 128), F32)),
        in_specs=[hbm, hbm, hbm, hbm, vmem, smem, hbm, hbm, hbm, hbm],
        out_specs=(vmem, vmem),
        scratch_shapes=[
            *[pltpu.VMEM((ROWS, COLS), F32)] * 4,
            *[pltpu.VMEM((ROWS, COLS), BF16)] * 3,
            pltpu.VMEM((16, TOK, 256), BF16),
            pltpu.VMEM((COLS, ROWS), BF16),
            pltpu.VMEM((32, PART, 128), BF16),
            pltpu.VMEM((2, COLS, ROWS), BF16),
            pltpu.VMEM((4, 2, PART, ROWS), BF16),
            pltpu.VMEM((4, 8, ROWS), F32),
            pltpu.VMEM((3, 8, 8, 128), F32),
            pltpu.VMEM((3, 8, 8, 128), F32),
            pltpu.VMEM((PART, TOK), F32),
            pltpu.VMEM((PART, TOK), BF16),
            pltpu.VMEM((4, 4, 2, PART, 128), BF16),
            pltpu.VMEM((4, 4, PART, 128), BF16),
            *[pltpu.VMEM((4, PART, 128), BF16)] * 7,
            pltpu.VMEM((COLS, ROWS), BF16),
            pltpu.SemaphoreType.DMA((12,)),
            pltpu.SemaphoreType.DMA((N_SEMS,)),
            pltpu.SemaphoreType.DMA((N_SEMS,)),
        ],
        compiler_params=pltpu.CompilerParams(
            collective_id=0, has_side_effects=True, vmem_limit_bytes=60 * 2**20
        ),
    )(
        tokens,
        gate_pre,
        up_act,
        hidden_cot,
        source_ids.reshape(1, ROWS),
        data_weight,
        grad,
        moment_m,
        moment_v,
        val_adjoint,
    )
    return curvature, sums[0, :NSRC]


def solution(mesh):
    split = P("dp", "tensor")
    in_specs = (split, split, split, split, P("dp"), P(), split, split, split, split)
    return jax.shard_map(body, mesh=mesh, in_specs=in_specs, out_specs=(split, P()), check_vma=False)
```

```python
import contextlib

import jax
import jax.numpy as jnp
from jax import lax
from jax.experimental import pallas as pl
from jax.experimental.pallas import tpu as pltpu
from jax.sharding import PartitionSpec as P

CLIP_NORM = 1.0
LEARN_RATE = 0.00015
BETA_ONE = 0.9
BETA_TWO = 0.95
ADAM_EPSILON = 1e-08
NORM_EPSILON = 1e-06

MESH = pl.DeviceIdType.MESH
BF16 = jnp.bfloat16
F32 = jnp.float32

ROWS = 128
COLS = 1792
PART = 448
TOK = 512
TOKENS = 4096
NSRC = 64


def mark(name):
    return contextlib.nullcontext()


class Slots:
    def __init__(self):
        self.used = 0

    def take(self, count):
        first = self.used
        self.used += count
        return first


RECV = Slots()
TZ = RECV.take(7)
TY = RECV.take(8)
TY_AHEAD = RECV.take(1)
TY_RELAY = RECV.take(1)
XZ = RECV.take(4)
XX = RECV.take(12)
XC = RECV.take(1)
AZ = RECV.take(2)
IZ = RECV.take(1)
N1 = RECV.take(3)
CC = RECV.take(16)
RX = RECV.take(12)
RZ = RECV.take(1)
N2 = RECV.take(3)
SEND = Slots()
S_TZ = SEND.take(1)
S_TY = SEND.take(1)
S_X = SEND.take(1)
S_A = SEND.take(2)
S_I = SEND.take(1)
S_N1 = SEND.take(3)
S_CC = SEND.take(1)
S_R = SEND.take(1)
S_Z = SEND.take(1)
S_N2 = SEND.take(3)


def kernel(
    tokens, gate, up, hid, ids, weight, grad, mom, sec, adj,
    res, src_out,
    grad_v, mom_v, sec_v, adj_v, gate_v, up_v, hid_v,
    tok, tang, xb, acts, act, idb, norm1, norm2, proj, mixed, cb, cr, s0, s1, s2, r0, r1, r2, fin,
    ls, ss, rs,
):
    dp, tn = lax.axis_index("dp"), lax.axis_index("tensor")
    zh, x, c = lax.div(dp, 8), lax.rem(lax.div(dp, 2), 4), lax.rem(dp, 2)
    zl, y = lax.div(tn, 4), lax.rem(tn, 4)
    z = zh * 2 + zl
    way = 1 - 2 * c

    def dev(z_at, x_at, y_at, c_at):
        return (lax.div(z_at, 2) * 8 + x_at * 2 + c_at, lax.rem(z_at, 2) * 4 + y_at)

    def zs(k):
        return lax.rem(z + k * way + 8, 8)

    def xs(k):
        return lax.rem(x + k * way + 4, 4)

    def ys(k):
        return lax.rem(y + k * way + 4, 4)

    def zhs(k):
        return lax.rem(zh + k + 4, 4)

    def at_zh(zh_at):
        return (zh_at * 8 + x * 2 + c, tn)

    x_dev = {k: dev(z, xs(k), y, c) for k in (1, -1)}
    y_dev = {k: dev(z, x, ys(k), c) for k in (1, -1)}
    z_dev = {k: dev(zs(k), x, y, c) for k in (1, -1)}
    core = dev(z, x, y, 1 - c)

    groups = (
        [dev(z, x, lax.rem(y + d, 4), c) for d in range(1, 4)],
        [dev(lax.rem(z + d, 8), x, y, c) for d in range(1, 8)],
        [dev(z, lax.div(lax.rem(x * 2 + c + d, 8), 2), y, lax.rem(c + d, 2)) for d in range(1, 8)],
    )
    places = (y, z, x * 2 + c)

    def push(src, dst, send, recv, to):
        pltpu.make_async_remote_copy(
            src_ref=src, dst_ref=dst, send_sem=ss.at[send], recv_sem=rs.at[recv], device_id=to, device_id_type=MESH
        ).start()

    def counted(ref, send, recv):
        return pltpu.make_async_remote_copy(
            src_ref=ref, dst_ref=ref, send_sem=ss.at[send], recv_sem=rs.at[recv], device_id=core, device_id_type=MESH
        )

    def arrived(ref, recv):
        counted(ref, 0, recv).wait_recv()

    def drained(ref, send):
        counted(ref, send, 0).wait_send()

    local = []

    def fetch(src, dst):
        copy = pltpu.make_async_copy(src, dst, ls.at[len(local)])
        copy.start()
        local.append(copy)
        return copy

    def shard(z_at, y_at):
        block = lax.rem(z_at, 2) * 4 + y_at
        return tok.at[pl.ds(2 * block, 2), pl.ds(pl.multiple_of(lax.div(z_at, 2) * ROWS, ROWS), ROWS), :]

    def spread(buf, send, recv, stage, value):
        place = places[stage]
        buf[stage, place] = value
        for to in groups[stage]:
            push(buf.at[stage, place], buf.at[stage, place], send + stage, recv + stage, to)

    def collect(buf, recv, stage):
        size = len(groups[stage]) + 1
        arrived(buf.at[stage, pl.ds(0, size - 1)], recv + stage)
        total = buf[stage, 0]
        for k in range(1, size):
            total = total + buf[stage, k]
        return total

    get_grad = fetch(grad, grad_v)
    block = zl * 4 + y
    own_rows = pl.ds(pl.multiple_of(zh * ROWS, ROWS), ROWS)
    get_tok = [fetch(tokens.at[:, pl.ds(h * 256, 256)], tok.at[2 * block + h, own_rows, :]) for h in range(2)]
    get_acts = [fetch(gate, gate_v), fetch(up, up_v), fetch(hid, hid_v)]
    get_rest = [fetch(mom, mom_v), fetch(sec, sec_v), fetch(adj, adj_v)]

    with mark("barrier"):
        barrier = pltpu.get_barrier_semaphore()
        for group in groups:
            for to in group:
                pl.semaphore_signal(barrier, inc=1, device_id=to, device_id_type=MESH)
        pl.semaphore_wait(barrier, sum(len(group) for group in groups))

    get_grad.wait()

    def square(k, total):
        part = grad_v[pl.ds(pl.multiple_of(k * 8, 8), 8), :]
        part = part * part
        for j in range(COLS // 128):
            total = total + part[:, j * 128 : (j + 1) * 128]
        return total

    with mark("squares"):
        spread(norm1, S_N1, N1, 0, lax.fori_loop(0, ROWS // 8, square, jnp.zeros((8, 128), F32)))

    for copy in get_tok:
        copy.wait()

    def pass_y(m, z_at):
        here = shard(z_at, y)
        push(here, here, S_TY, TY + m, y_dev[1])
        push(here, here, S_TY, TY_AHEAD, y_dev[-1])

    def relay_y(m, z_at):
        with mark(f"ry{m}"):
            there = shard(z_at, ys(-1))
            arrived(there, TY + m)
            push(there, there, S_TY, TY_RELAY, y_dev[1])

    own = shard(z, y)
    push(own, own, S_TZ, TZ, z_dev[1])
    push(own, own, S_TZ, TZ + 4, z_dev[-1])
    pass_y(0, z)

    for copy in get_acts:
        copy.wait()
    ids_row = ids[...]
    weight_row = jnp.zeros((1, ROWS), F32)
    for k in range(NSRC):
        weight_row = jnp.where(ids_row == k, weight[k], weight_row)
    weight_row = weight_row / TOKENS
    idb[zh] = jnp.broadcast_to(ids_row.astype(F32), (8, ROWS))

    def activation(j, carry):
        cols = pl.ds(pl.multiple_of(j * 128, 128), 128)
        pre = gate_v[:, cols].astype(F32)
        sigma = 1.0 / (1.0 + jnp.exp(-pre))
        coupling = up_v[:, cols].astype(F32) * hid_v[:, cols].astype(F32)
        first = coupling * sigma * (1.0 + pre * (1.0 - sigma))
        second = coupling * sigma * (1.0 - sigma) * (2.0 + pre * (1.0 - 2.0 * sigma))
        acts[0, cols, :] = first.T.astype(BF16)
        acts[1, cols, :] = (second.T * weight_row).astype(BF16)
        return carry

    with mark("activation"):
        lax.fori_loop(0, COLS // 128, activation, 0)

    def part_rows(q):
        return pl.ds(pl.multiple_of(q * PART, 64), PART)

    def share_acts(which):
        for d in (2, 1, 3):
            push(acts.at[which, part_rows(zhs(d)), :], act.at[which, zh], S_A + which, AZ + which, at_zh(zhs(d)))

    for d in (1, 2, 3):
        push(idb.at[zh], idb.at[zh], S_I, IZ, at_zh(zhs(d)))
    keep_act = [fetch(acts.at[k, part_rows(zh), :], act.at[k, zh]) for k in range(2)]

    with mark("norm_a"):
        spread(norm1, S_N1, N1, 1, collect(norm1, N1, 0))

    def forward_z(k):
        with mark(f"fz{k}"):
            z_at = zs(-k)
            arrived(shard(z_at, y), TZ + k - 1)
            if k < 4:
                push(shard(z_at, y), shard(z_at, y), S_TZ, TZ + k, z_dev[1])
            pass_y(2 * k - 1, z_at)

    def backward_z(k):
        with mark(f"bz{k}"):
            z_at = zs(k)
            arrived(shard(z_at, y), TZ + 4 + k - 1)
            if k < 3:
                push(shard(z_at, y), shard(z_at, y), S_TZ, TZ + 4 + k, z_dev[-1])
            pass_y(2 * k, z_at)

    forward_z(1)
    backward_z(1)
    with mark("norm_b"):
        spread(norm1, S_N1, N1, 2, collect(norm1, N1, 1))
    relay_y(0, z)
    forward_z(2)
    backward_z(2)
    with mark("norm_c"):
        total_sq = jnp.sum(collect(norm1, N1, 2), keepdims=True) + NORM_EPSILON
    clip = jnp.minimum(CLIP_NORM * lax.rsqrt(total_sq), 1.0)
    for copy in get_rest:
        copy.wait()

    def tangent(j, carry):
        cols = pl.ds(pl.multiple_of(j * 128, 128), 128)
        clipped = clip * grad_v[:, cols]
        moment_new = BETA_ONE * mom_v[:, cols] + (1.0 - BETA_ONE) * clipped
        second_new = BETA_TWO * sec_v[:, cols] + (1.0 - BETA_TWO) * clipped * clipped
        root_v = jnp.sqrt(second_new)
        inverse = 1.0 / (root_v + ADAM_EPSILON)
        jacobian = -LEARN_RATE * (
            (1.0 - BETA_ONE) * inverse - moment_new * (1.0 - BETA_TWO) * clipped * (inverse * inverse / root_v)
        )
        pulled = jacobian * adj_v[:, cols]
        tang[cols, :] = (clip * pulled).T.astype(BF16)
        return carry

    with mark("tangent"):
        lax.fori_loop(0, COLS // 128, tangent, 0)

    keep = fetch(tang.at[part_rows(zh), :], xb.at[dp])
    forward_z(3)
    backward_z(3)
    for d in (1, 3, 2):
        push(tang.at[part_rows(zhs(d)), :], xb.at[dp], S_X, XZ + d, at_zh(zhs(d)))

    def x_block(x_at, d):
        return xb.at[zhs(-d) * 8 + x_at * 2 + c]

    def x_own(d):
        with mark(f"xown{d}"):
            here = x_block(x, d)
            if d:
                arrived(here, XZ + d)
            else:
                keep.wait()
            push(here, here, S_X, XX + d, x_dev[1])
            push(here, here, S_X, XX + 4 + d, x_dev[-1])
            push(here, here, S_X, XC, core)

    def x_sides(d):
        with mark(f"xside{d}"):
            there = x_block(xs(-1), d)
            arrived(there, XX + d)
            push(there, there, S_X, XX + 8 + d, x_dev[1])
            push(there, there, S_X, XC, core)
            there = x_block(xs(1), d)
            arrived(there, XX + 4 + d)
            push(there, there, S_X, XC, core)

    def x_relay(d):
        with mark(f"xrelay{d}"):
            there = x_block(xs(2), d)
            arrived(there, XX + 8 + d)
            push(there, there, S_X, XC, core)

    x_own(0)
    relay_y(1, zs(-1))
    relay_y(2, zs(1))
    x_sides(0)
    relay_y(3, zs(-2))
    forward_z(4)
    x_own(1)
    x_own(3)
    x_relay(0)
    relay_y(4, zs(2))
    x_own(2)
    share_acts(1)
    share_acts(0)
    x_sides(1)
    x_sides(3)
    relay_y(5, zs(-3))
    x_relay(1)
    x_relay(3)
    x_sides(2)
    relay_y(6, zs(3))
    x_relay(2)
    relay_y(7, zs(-4))

    with mark("ylast"):
        arrived(tok.at[pl.ds(0, 4)], TY_AHEAD)
        arrived(tok.at[pl.ds(0, 4)], TY_RELAY)
    with mark("xcore"):
        arrived(xb.at[pl.ds(0, 16)], XC)

    proj[...] = jnp.zeros_like(proj)

    def first_product(k, carry):
        left = jnp.concatenate([xb[8 * k + i] for i in range(8)], axis=1)
        right = jnp.concatenate([tok[4 * k + i] for i in range(4)], axis=1)
        proj[...] += lax.dot_general(left, right, (((1,), (1,)), ((), ())), preferred_element_type=F32)
        return carry

    with mark("product1"):
        lax.fori_loop(0, 4, first_product, 0)

    with mark("second_wait"):
        for copy in keep_act:
            copy.wait()
        arrived(act.at[1, pl.ds(0, 3)], AZ + 1)

    with mark("mix"):
        for k in range(4):
            cols = pl.ds(k * ROWS, ROWS)
            mixed[:, cols] = (proj[:, cols] * act[1, k].astype(F32)).astype(BF16)

    def source_sums():
        arrived(act.at[0, pl.ds(0, 3)], AZ)
        arrived(idb.at[pl.ds(0, 3)], IZ)
        sums = jnp.zeros((8, 128), F32)
        source = lax.broadcasted_iota(jnp.int32, (128, ROWS), 0).astype(F32)
        for k in range(4):
            part = proj[:, pl.ds(k * ROWS, ROWS)]
            per_tok = jnp.sum(part * act[0, k].astype(F32), axis=0, keepdims=True)
            onehot = (source == idb[k, 0:1, :]).astype(F32)
            sums = sums + lax.dot_general(
                jnp.broadcast_to(per_tok, (8, ROWS)),
                onehot,
                (((1,), (1,)), ((), ())),
                precision=lax.Precision.HIGHEST,
                preferred_element_type=F32,
            )
        return sums

    order = (2, 1, 3, 0)
    behind, ahead = 3 - 2 * c, 1 + 2 * c

    def second_product(offset, j):
        x_at, zh_at = lax.rem(x + offset, 4), zhs(order[j])
        whole = jnp.dot(mixed[...], tok[zh_at * 4 + x_at], preferred_element_type=F32)
        cb[x_at, zh_at, 0] = whole[:, :128].astype(BF16)
        cb[x_at, zh_at, 1] = whole[:, 128:].astype(BF16)
        push(cb.at[x_at, zh_at, 1 - c], cr.at[x_at, zh_at], S_CC, CC + offset * 4 + j, core)

    def both(offset, j):
        x_at, zh_at = lax.rem(x + offset, 4), zhs(order[j])
        arrived(cr.at[x_at, zh_at], CC + offset * 4 + j)
        return cb[x_at, zh_at, c].astype(F32) + cr[x_at, zh_at].astype(F32)

    def opposite(j):
        with mark(f"opposite{j}"):
            s0[j] = both(2, j).astype(BF16)
            push(s0.at[j], r0.at[j], S_R, RX + j, x_dev[1])

    def backward(j):
        with mark(f"backward{j}"):
            s2[j] = both(behind, j).astype(BF16)
            push(s2.at[j], r2.at[j], S_R, RX + 8 + j, x_dev[-1])

    def onward(j):
        with mark(f"onward{j}"):
            part = both(ahead, j)
            arrived(r0.at[j], RX + j)
            s1[j] = (part + r0[j].astype(F32)).astype(BF16)
            push(s1.at[j], r1.at[j], S_R, RX + 4 + j, x_dev[1])

    def finish(j):
        with mark(f"finish{j}"):
            part = both(0, j)
            arrived(r2.at[j], RX + 8 + j)
            part = part + r2[j].astype(F32)
            arrived(r1.at[j], RX + 4 + j)
            fin[j] = (part + r1[j].astype(F32)).astype(BF16)
            d = order[j]
            if d:
                push(fin.at[j], res.at[part_rows(zh), :], S_Z, RZ, at_zh(zhs(d)))
            else:
                fetch(fin.at[j], res.at[part_rows(zh), :])

    todo = (
        (2, 0), (1, 0), (3, 0), (2, 1), (1, 1), (3, 1), (2, 2), (0, 0), (1, 2), (3, 2), (2, 3), (0, 1), (1, 3), (3, 3), (0, 2), (0, 3),
    )
    then = {
        4: [(opposite, 0)], 6: [(backward, 0)], 7: [(opposite, 1)], 9: [(backward, 1)], 10: [(opposite, 2)],
        12: [(onward, 0)], 13: [(backward, 2)], 14: [(opposite, 3)], 15: [(onward, 1), (backward, 3)],
    }
    for i, (offset, j) in enumerate(todo):
        with mark(f"second{i}"):
            second_product(offset, j)
        for step, at in then.get(i, ()):
            step(at)
    with mark("n2_0"):
        spread(norm2, S_N2, N2, 0, source_sums())
    onward(2)
    with mark("n2_1"):
        spread(norm2, S_N2, N2, 1, collect(norm2, N2, 0))
    finish(0)
    onward(3)
    finish(1)
    with mark("n2_2"):
        spread(norm2, S_N2, N2, 2, collect(norm2, N2, 1))
    finish(2)
    finish(3)
    with mark("zlast"):
        arrived(cr.at[0, pl.ds(0, 3)], RZ)
    with mark("n2_3"):
        src_out[...] = collect(norm2, N2, 2) / TOKENS
    with mark("drain"):
        local[-1].wait()
        drained(tok.at[pl.ds(0, 7), pl.ds(0, 256)], S_TZ)
        drained(tok.at[pl.ds(0, 12)], S_TY)
        drained(xb.at[pl.ds(0, 31)], S_X)
        for which in range(2):
            drained(act.at[which, pl.ds(0, 3)], S_A + which)
        drained(idb.at[pl.ds(0, 3)], S_I)
        drained(cr, S_CC)
        drained(cr.at[pl.ds(0, 3)], S_R)
        drained(cr.at[0, pl.ds(0, 3)], S_Z)
        for stage in range(3):
            drained(norm1.at[0, pl.ds(0, len(groups[stage]))], S_N1 + stage)
            drained(norm2.at[0, pl.ds(0, len(groups[stage]))], S_N2 + stage)


def emit(res, sums, out, src):
    def turn(j, carry):
        cols = pl.ds(pl.multiple_of(j * 128, 128), 128)
        out[:, cols] = res[cols, :].astype(F32).T
        return carry

    lax.fori_loop(0, COLS // 128, turn, 0, unroll=2)
    src[...] = sums[0:1, :NSRC]


def body(tokens, gate_pre, up_act, hidden_cot, source_ids, data_weight, grad, moment_m, moment_v, val_adjoint):
    hbm = pl.BlockSpec(memory_space=pl.ANY)
    vmem = pl.BlockSpec(memory_space=pltpu.VMEM)
    smem = pl.BlockSpec(memory_space=pltpu.SMEM)
    turned, sums = pl.pallas_call(
        kernel,
        name="metagradient",
        out_shape=(jax.ShapeDtypeStruct((COLS, ROWS), BF16), jax.ShapeDtypeStruct((8, 128), F32)),
        in_specs=[hbm, hbm, hbm, hbm, vmem, smem, hbm, hbm, hbm, hbm],
        out_specs=(hbm, vmem),
        scratch_shapes=[
            *[pltpu.VMEM((ROWS, COLS), F32)] * 4,
            *[pltpu.VMEM((ROWS, COLS), BF16)] * 3,
            pltpu.VMEM((16, TOK, 256), BF16),
            pltpu.VMEM((COLS, ROWS), BF16),
            pltpu.VMEM((32, PART, 128), BF16),
            pltpu.VMEM((2, COLS, ROWS), BF16),
            pltpu.VMEM((2, 4, PART, ROWS), BF16),
            pltpu.VMEM((4, 8, ROWS), F32),
            pltpu.VMEM((3, 8, 8, 128), F32),
            pltpu.VMEM((3, 8, 8, 128), F32),
            pltpu.VMEM((PART, TOK), F32),
            pltpu.VMEM((PART, TOK), BF16),
            pltpu.VMEM((4, 4, 2, PART, 128), BF16),
            pltpu.VMEM((4, 4, PART, 128), BF16),
            *[pltpu.VMEM((4, PART, 128), BF16)] * 7,
            pltpu.SemaphoreType.DMA((14,)),
            pltpu.SemaphoreType.DMA((SEND.used,)),
            pltpu.SemaphoreType.DMA((RECV.used,)),
        ],
        compiler_params=pltpu.CompilerParams(
            collective_id=0, has_side_effects=True, vmem_limit_bytes=60 * 2**20
        ),
    )(
        tokens,
        gate_pre,
        up_act,
        hidden_cot,
        source_ids.reshape(1, ROWS),
        data_weight,
        grad,
        moment_m,
        moment_v,
        val_adjoint,
    )
    curvature, source_grad = pl.pallas_call(
        emit,
        name="emit",
        out_shape=(jax.ShapeDtypeStruct((ROWS, COLS), F32), jax.ShapeDtypeStruct((1, NSRC), F32)),
        in_specs=[vmem, vmem],
        out_specs=(vmem, vmem),
        compiler_params=pltpu.CompilerParams(vmem_limit_bytes=60 * 2**20),
    )(turned, sums)
    return curvature, source_grad.reshape(NSRC)


def solution(mesh):
    split = P("dp", "tensor")
    in_specs = (split, split, split, split, P("dp"), P(), split, split, split, split)
    return jax.shard_map(body, mesh=mesh, in_specs=in_specs, out_specs=(split, P()), check_vma=False)
```

```python
import contextlib

import jax
import jax.numpy as jnp
from jax import lax
from jax.experimental import pallas as pl
from jax.experimental.pallas import tpu as pltpu
from jax.sharding import PartitionSpec as P

CLIP_NORM = 1.0
LEARN_RATE = 0.00015
BETA_ONE = 0.9
BETA_TWO = 0.95
ADAM_EPSILON = 1e-08
NORM_EPSILON = 1e-06

MESH = pl.DeviceIdType.MESH
BF16 = jnp.bfloat16
F32 = jnp.float32

ROWS = 128
COLS = 1792
PART = 448
HALF = 224
TOK = 512
TOKENS = 4096
NSRC = 64


def mark(name):
    return contextlib.nullcontext()


class Slots:
    def __init__(self):
        self.used = 0

    def take(self, count):
        first = self.used
        self.used += count
        return first


RECV = Slots()
TZ = RECV.take(7)
TY = RECV.take(8)
TY_AHEAD = RECV.take(1)
TY_RELAY = RECV.take(1)
XZ = RECV.take(4)
XX = RECV.take(12)
XC = RECV.take(1)
AZ = RECV.take(2)
IZ = RECV.take(1)
N1 = RECV.take(3)
CC = RECV.take(16)
RX = RECV.take(24)
RZ = RECV.take(1)
N2 = RECV.take(3)
SEND = Slots()
S_TZ = SEND.take(1)
S_TY = SEND.take(1)
S_X = SEND.take(1)
S_A = SEND.take(2)
S_I = SEND.take(1)
S_N1 = SEND.take(3)
S_CC = SEND.take(1)
S_R = SEND.take(1)
S_Z = SEND.take(1)
S_N2 = SEND.take(3)


def kernel(
    tokens, gate, up, hid, ids, weight, grad, mom, sec, adj,
    res, src_out,
    grad_v, mom_v, sec_v, adj_v, gate_v, up_v, hid_v,
    tok, tang, xb, acts, act, idb, norm1, norm2, proj, mixed, cb, cr, s0, s1, s2, r0, r1, r2, fin,
    ids_v, weight_s, sums,
    ls, ss, rs,
):
    dp, tn = lax.axis_index("dp"), lax.axis_index("tensor")
    zh, x, c = lax.div(dp, 8), lax.rem(lax.div(dp, 2), 4), lax.rem(dp, 2)
    zl, y = lax.div(tn, 4), lax.rem(tn, 4)
    z = zh * 2 + zl
    way = 1 - 2 * c

    def dev(z_at, x_at, y_at, c_at):
        return (lax.div(z_at, 2) * 8 + x_at * 2 + c_at, lax.rem(z_at, 2) * 4 + y_at)

    def zs(k):
        return lax.rem(z + k * way + 8, 8)

    def xs(k):
        return lax.rem(x + k * way + 4, 4)

    def ys(k):
        return lax.rem(y + k * way + 4, 4)

    def zhs(k):
        return lax.rem(zh + k + 4, 4)

    def at_zh(zh_at):
        return (zh_at * 8 + x * 2 + c, tn)

    x_dev = {k: dev(z, xs(k), y, c) for k in (1, -1)}
    y_dev = {k: dev(z, x, ys(k), c) for k in (1, -1)}
    z_dev = {k: dev(zs(k), x, y, c) for k in (1, -1)}
    core = dev(z, x, y, 1 - c)

    groups = (
        [dev(z, x, lax.rem(y + d, 4), c) for d in range(1, 4)],
        [dev(lax.rem(z + d, 8), x, y, c) for d in range(1, 8)],
        [dev(z, lax.div(lax.rem(x * 2 + c + d, 8), 2), y, lax.rem(c + d, 2)) for d in range(1, 8)],
    )
    places = (y, z, x * 2 + c)

    def push(src, dst, send, recv, to):
        pltpu.make_async_remote_copy(
            src_ref=src, dst_ref=dst, send_sem=ss.at[send], recv_sem=rs.at[recv], device_id=to, device_id_type=MESH
        ).start()

    def counted(ref, send, recv):
        return pltpu.make_async_remote_copy(
            src_ref=ref, dst_ref=ref, send_sem=ss.at[send], recv_sem=rs.at[recv], device_id=core, device_id_type=MESH
        )

    def arrived(ref, recv):
        counted(ref, 0, recv).wait_recv()

    def drained(ref, send):
        counted(ref, send, 0).wait_send()

    local = []

    def fetch(src, dst):
        copy = pltpu.make_async_copy(src, dst, ls.at[len(local)])
        copy.start()
        local.append(copy)
        return copy

    def shard(z_at, y_at):
        block = lax.rem(z_at, 2) * 4 + y_at
        return tok.at[pl.ds(2 * block, 2), pl.ds(pl.multiple_of(lax.div(z_at, 2) * ROWS, ROWS), ROWS), :]

    def spread(buf, send, recv, stage, value):
        place = places[stage]
        buf[stage, place] = value
        for to in groups[stage]:
            push(buf.at[stage, place], buf.at[stage, place], send + stage, recv + stage, to)

    def collect(buf, recv, stage):
        size = len(groups[stage]) + 1
        arrived(buf.at[stage, pl.ds(0, size - 1)], recv + stage)
        total = buf[stage, 0]
        for k in range(1, size):
            total = total + buf[stage, k]
        return total

    get_grad = fetch(grad, grad_v)
    with mark("barrier"):
        barrier = pltpu.get_barrier_semaphore()
        for group in (groups[1], groups[0], groups[2]):
            for to in group:
                pl.semaphore_signal(barrier, inc=1, device_id=to, device_id_type=MESH)
    block = zl * 4 + y
    own_rows = pl.ds(pl.multiple_of(zh * ROWS, ROWS), ROWS)
    get_tok = [fetch(tokens.at[:, pl.ds(h * 256, 256)], tok.at[2 * block + h, own_rows, :]) for h in range(2)]
    get_acts = [fetch(gate, gate_v), fetch(up, up_v), fetch(hid, hid_v), fetch(ids, ids_v), fetch(weight, weight_s)]
    get_rest = [fetch(mom, mom_v), fetch(sec, sec_v), fetch(adj, adj_v)]
    with mark("barrier_wait"):
        pl.semaphore_wait(barrier, sum(len(group) for group in groups))

    get_grad.wait()

    def square(k, total):
        part = grad_v[pl.ds(pl.multiple_of(k * 8, 8), 8), :]
        part = part * part
        for j in range(COLS // 128):
            total = total + part[:, j * 128 : (j + 1) * 128]
        return total

    with mark("squares"):
        spread(norm1, S_N1, N1, 0, lax.fori_loop(0, ROWS // 8, square, jnp.zeros((8, 128), F32)))

    for copy in get_tok:
        copy.wait()

    def pass_y(m, z_at):
        here = shard(z_at, y)
        push(here, here, S_TY, TY + m, y_dev[1])
        push(here, here, S_TY, TY_AHEAD, y_dev[-1])

    def relay_y(m, z_at):
        with mark(f"ry{m}"):
            there = shard(z_at, ys(-1))
            arrived(there, TY + m)
            push(there, there, S_TY, TY_RELAY, y_dev[1])

    own = shard(z, y)
    push(own, own, S_TZ, TZ, z_dev[1])
    push(own, own, S_TZ, TZ + 4, z_dev[-1])
    pass_y(0, z)

    for copy in get_acts:
        copy.wait()
    ids_row = ids_v[...]
    weight_row = jnp.zeros((1, ROWS), F32)
    for k in range(NSRC):
        weight_row = jnp.where(ids_row == k, weight_s[k], weight_row)
    weight_row = weight_row / TOKENS
    idb[zh] = jnp.broadcast_to(ids_row.astype(F32), (8, ROWS))

    def activation(j, carry):
        cols = pl.ds(pl.multiple_of(j * 128, 128), 128)
        pre = gate_v[:, cols].astype(F32)
        sigma = 1.0 / (1.0 + jnp.exp(-pre))
        coupling = up_v[:, cols].astype(F32) * hid_v[:, cols].astype(F32)
        first = coupling * sigma * (1.0 + pre * (1.0 - sigma))
        second = coupling * sigma * (1.0 - sigma) * (2.0 + pre * (1.0 - 2.0 * sigma))
        acts[0, cols, :] = first.T.astype(BF16)
        acts[1, cols, :] = (second.T * weight_row).astype(BF16)
        return carry

    with mark("activation"):
        lax.fori_loop(0, COLS // 128, activation, 0)

    def part_rows(q):
        return pl.ds(pl.multiple_of(q * PART, 64), PART)

    def share_acts(which):
        for d in (2, 1, 3):
            push(acts.at[which, part_rows(zhs(d)), :], act.at[which, zh], S_A + which, AZ + which, at_zh(zhs(d)))

    for d in (1, 2, 3):
        push(idb.at[zh], idb.at[zh], S_I, IZ, at_zh(zhs(d)))
    keep_act = [fetch(acts.at[k, part_rows(zh), :], act.at[k, zh]) for k in range(2)]

    def forward_z(k):
        with mark(f"fz{k}"):
            z_at = zs(-k)
            arrived(shard(z_at, y), TZ + k - 1)
            if k < 4:
                push(shard(z_at, y), shard(z_at, y), S_TZ, TZ + k, z_dev[1])
            pass_y(2 * k - 1, z_at)

    def backward_z(k):
        with mark(f"bz{k}"):
            z_at = zs(k)
            arrived(shard(z_at, y), TZ + 4 + k - 1)
            if k < 3:
                push(shard(z_at, y), shard(z_at, y), S_TZ, TZ + 4 + k, z_dev[-1])
            pass_y(2 * k, z_at)

    with mark("norm_a"):
        spread(norm1, S_N1, N1, 1, collect(norm1, N1, 0))
    forward_z(1)
    backward_z(1)
    with mark("norm_b"):
        spread(norm1, S_N1, N1, 2, collect(norm1, N1, 1))
    relay_y(0, z)
    forward_z(2)
    backward_z(2)
    with mark("norm_c"):
        total_sq = jnp.sum(collect(norm1, N1, 2), keepdims=True) + NORM_EPSILON
    clip = jnp.minimum(CLIP_NORM * lax.rsqrt(total_sq), 1.0)
    for copy in get_rest:
        copy.wait()

    def tangent(q):
        first = lax.div(7 * q, 2)

        def tile(j, carry):
            cols = pl.ds(pl.multiple_of((first + j) * 128, 128), 128)
            clipped = clip * grad_v[:, cols]
            moment_new = BETA_ONE * mom_v[:, cols] + (1.0 - BETA_ONE) * clipped
            second_new = BETA_TWO * sec_v[:, cols] + (1.0 - BETA_TWO) * clipped * clipped
            root_v = jnp.sqrt(second_new)
            inverse = 1.0 / (root_v + ADAM_EPSILON)
            jacobian = -LEARN_RATE * (
                (1.0 - BETA_ONE) * inverse - moment_new * (1.0 - BETA_TWO) * clipped * (inverse * inverse / root_v)
            )
            pulled = jacobian * adj_v[:, cols]
            tang[q, pl.ds(pl.multiple_of(j * 128, 128), 128), :] = (clip * pulled).T.astype(BF16)
            return carry

        lax.fori_loop(0, 4, tile, 0)
        return tang.at[q, pl.ds(pl.multiple_of(lax.rem(q, 2) * 64, 64), PART), :]

    def x_first(d):
        with mark(f"tangent{d}"):
            push(tangent(zhs(d)), xb.at[dp], S_X, XZ + d, at_zh(zhs(d)))

    x_first(1)
    x_first(3)
    x_first(2)
    with mark("tangent0"):
        keep = fetch(tangent(zh), xb.at[dp])
    relay_y(1, zs(-1))
    relay_y(2, zs(1))

    def x_block(x_at, d):
        return xb.at[zhs(-d) * 8 + x_at * 2 + c]

    def x_own(d):
        with mark(f"xown{d}"):
            here = x_block(x, d)
            if d:
                arrived(here, XZ + d)
            else:
                keep.wait()
            push(here, here, S_X, XX + d, x_dev[1])
            push(here, here, S_X, XX + 4 + d, x_dev[-1])
            push(here, here, S_X, XC, core)

    def x_sides(d):
        with mark(f"xside{d}"):
            there = x_block(xs(-1), d)
            arrived(there, XX + d)
            push(there, there, S_X, XX + 8 + d, x_dev[1])
            push(there, there, S_X, XC, core)
            there = x_block(xs(1), d)
            arrived(there, XX + 4 + d)
            push(there, there, S_X, XC, core)

    def x_relay(d):
        with mark(f"xrelay{d}"):
            there = x_block(xs(2), d)
            arrived(there, XX + 8 + d)
            push(there, there, S_X, XC, core)

    x_own(0)
    forward_z(3)
    backward_z(3)
    x_sides(0)
    x_own(1)
    x_own(3)
    share_acts(1)
    relay_y(3, zs(-2))
    relay_y(4, zs(2))
    x_relay(0)
    x_own(2)
    x_sides(1)
    x_sides(3)
    forward_z(4)
    relay_y(5, zs(-3))
    relay_y(6, zs(3))
    x_sides(2)
    x_relay(1)
    x_relay(3)
    relay_y(7, zs(-4))
    share_acts(0)
    x_relay(2)

    proj[...] = jnp.zeros_like(proj)

    def first_product(y_at):
        left = jnp.concatenate([xb[4 * k + i] for k in (y_at, y_at + 4) for i in range(4)], axis=1)
        right = jnp.concatenate([tok[2 * k + i] for k in (y_at, y_at + 4) for i in range(2)], axis=1)
        proj[...] += lax.dot_general(left, right, (((1,), (1,)), ((), ())), preferred_element_type=F32)

    with mark("ynear"):
        arrived(tok.at[pl.ds(0, 4)], TY_AHEAD)
    with mark("xcore"):
        arrived(xb.at[pl.ds(0, 16)], XC)

    def near(k, carry):
        first_product(lax.rem(y + 3 + k, 4))
        return carry

    with mark("product1"):
        lax.fori_loop(0, 3, near, 0)
    with mark("yfar"):
        arrived(tok.at[pl.ds(0, 4)], TY_RELAY)

    with mark("product1b"):
        first_product(lax.rem(y + 2, 4))

    with mark("second_wait"):
        for copy in keep_act:
            copy.wait()
        arrived(act.at[1, pl.ds(0, 3)], AZ + 1)

    with mark("mix"):
        for k in range(4):
            cols = pl.ds(k * ROWS, ROWS)
            mixed[:, cols] = (proj[:, cols] * act[1, k].astype(F32)).astype(BF16)

    def source_sums():
        arrived(act.at[0, pl.ds(0, 3)], AZ)
        arrived(idb.at[pl.ds(0, 3)], IZ)
        total = jnp.zeros((8, 128), F32)
        source = lax.broadcasted_iota(jnp.int32, (128, ROWS), 0).astype(F32)
        for k in range(4):
            part = proj[:, pl.ds(k * ROWS, ROWS)]
            per_tok = jnp.sum(part * act[0, k].astype(F32), axis=0, keepdims=True)
            onehot = (source == idb[k, 0:1, :]).astype(F32)
            total = total + lax.dot_general(
                jnp.broadcast_to(per_tok, (8, ROWS)),
                onehot,
                (((1,), (1,)), ((), ())),
                precision=lax.Precision.HIGHEST,
                preferred_element_type=F32,
            )
        return total

    order = (2, 1, 3, 0)
    behind, ahead = 3 - 2 * c, 1 + 2 * c

    def second_product(offset, j):
        x_at, zh_at = lax.rem(x + offset, 4), zhs(order[j])
        whole = jnp.dot(mixed[...], tok[zh_at * 4 + x_at], preferred_element_type=F32)
        cb[x_at, zh_at, 0] = whole[:, :128].astype(BF16)
        cb[x_at, zh_at, 1] = whole[:, 128:].astype(BF16)
        push(cb.at[x_at, zh_at, 1 - c], cr.at[x_at, zh_at], S_CC, CC + offset * 4 + j, core)

    def half(h):
        return pl.ds(h * HALF, HALF)

    def both(offset, j, h):
        x_at, zh_at = lax.rem(x + offset, 4), zhs(order[j])
        if h == 0:
            arrived(cr.at[x_at, zh_at], CC + offset * 4 + j)
        return cb[x_at, zh_at, c, half(h)].astype(F32) + cr[x_at, zh_at, half(h)].astype(F32)

    def opposite(j, h):
        with mark(f"opposite{j}{h}"):
            s0[j, half(h)] = both(2, j, h).astype(BF16)
            push(s0.at[j, half(h)], r0.at[j, half(h)], S_R, RX + 2 * j + h, x_dev[1])

    def backward(j, h):
        with mark(f"backward{j}{h}"):
            s2[j, half(h)] = both(behind, j, h).astype(BF16)
            push(s2.at[j, half(h)], r2.at[j, half(h)], S_R, RX + 16 + 2 * j + h, x_dev[-1])

    def onward(j, h):
        with mark(f"onward{j}{h}"):
            part = both(ahead, j, h)
            arrived(r0.at[j, half(h)], RX + 2 * j + h)
            s1[j, half(h)] = (part + r0[j, half(h)].astype(F32)).astype(BF16)
            push(s1.at[j, half(h)], r1.at[j, half(h)], S_R, RX + 8 + 2 * j + h, x_dev[1])

    def finish(j, h):
        with mark(f"finish{j}{h}"):
            part = both(0, j, h)
            arrived(r2.at[j, half(h)], RX + 16 + 2 * j + h)
            part = part + r2[j, half(h)].astype(F32)
            arrived(r1.at[j, half(h)], RX + 8 + 2 * j + h)
            fin[j, half(h)] = (part + r1[j, half(h)].astype(F32)).astype(BF16)
            d = order[j]
            rows = pl.ds(pl.multiple_of(zh * PART + h * HALF, 32), HALF)
            if d:
                push(fin.at[j, half(h)], res.at[rows, :], S_Z, RZ, at_zh(zhs(d)))
            elif h:
                fetch(fin.at[j], res.at[part_rows(zh), :])

    todo = (
        (2, 0), (1, 0), (3, 0), (2, 1), (1, 1), (3, 1), (2, 2), (1, 2), (3, 2), (0, 0), (2, 3), (1, 3), (3, 3), (0, 1), (0, 2), (0, 3),
    )
    then = {
        4: [(opposite, 0, 0), (opposite, 0, 1)],
        6: [(backward, 0, 0), (backward, 0, 1)],
        8: [(opposite, 1, 0)],
        9: [(backward, 1, 0)],
        11: [(onward, 0, 0), (onward, 0, 1)],
        12: [(opposite, 2, 0), (backward, 2, 0)],
        13: [(opposite, 1, 1), (backward, 1, 1)],
        15: [(onward, 1, 0), (opposite, 2, 1), (backward, 2, 1)],
    }
    for i, (offset, j) in enumerate(todo):
        with mark(f"second{i}"):
            second_product(offset, j)
        for step, at, h in then.get(i, ()):
            step(at, h)
    with mark("n2_0"):
        spread(norm2, S_N2, N2, 1, source_sums())
    finish(0, 0)
    finish(0, 1)
    onward(2, 0)
    onward(1, 1)
    opposite(3, 0)
    backward(3, 0)
    finish(1, 0)
    onward(2, 1)
    opposite(3, 1)
    backward(3, 1)
    with mark("n2_1"):
        spread(norm2, S_N2, N2, 0, collect(norm2, N2, 1))
    finish(2, 0)
    finish(1, 1)
    onward(3, 0)
    finish(2, 1)
    onward(3, 1)
    with mark("n2_2"):
        spread(norm2, S_N2, N2, 2, collect(norm2, N2, 0))
    finish(3, 0)
    finish(3, 1)
    with mark("zlast"):
        arrived(cr.at[0, pl.ds(0, 3)], RZ)
    with mark("n2_3"):
        sums[...] = collect(norm2, N2, 2) / TOKENS
        fetch(sums, src_out)
    with mark("drain"):
        local[-1].wait()
        local[-2].wait()
        drained(tok.at[pl.ds(0, 7), pl.ds(0, 256)], S_TZ)
        drained(tok.at[pl.ds(0, 12)], S_TY)
        drained(xb.at[pl.ds(0, 31)], S_X)
        for which in range(2):
            drained(act.at[which, pl.ds(0, 3)], S_A + which)
        drained(idb.at[pl.ds(0, 3)], S_I)
        drained(cr, S_CC)
        drained(cr.at[pl.ds(0, 3)], S_R)
        drained(cr.at[0, pl.ds(0, 3)], S_Z)
        for stage in range(3):
            drained(norm1.at[0, pl.ds(0, len(groups[stage]))], S_N1 + stage)
            drained(norm2.at[0, pl.ds(0, len(groups[stage]))], S_N2 + stage)


def emit(res, sums, out, src):
    def turn(j, carry):
        cols = pl.ds(pl.multiple_of(j * 128, 128), 128)
        out[:, cols] = res[cols, :].astype(F32).T
        return carry

    lax.fori_loop(0, COLS // 128, turn, 0, unroll=2)
    src[...] = sums[0:1, :NSRC]


def body(tokens, gate_pre, up_act, hidden_cot, source_ids, data_weight, grad, moment_m, moment_v, val_adjoint):
    hbm = pl.BlockSpec(memory_space=pl.ANY)
    vmem = pl.BlockSpec(memory_space=pltpu.VMEM)
    turned, sums = pl.pallas_call(
        kernel,
        name="metagradient",
        out_shape=(jax.ShapeDtypeStruct((COLS, ROWS), BF16), jax.ShapeDtypeStruct((8, 128), F32)),
        in_specs=[hbm] * 10,
        out_specs=(hbm, hbm),
        scratch_shapes=[
            *[pltpu.VMEM((ROWS, COLS), F32)] * 4,
            *[pltpu.VMEM((ROWS, COLS), BF16)] * 3,
            pltpu.VMEM((16, TOK, 256), BF16),
            pltpu.VMEM((4, 512, ROWS), BF16),
            pltpu.VMEM((32, PART, 128), BF16),
            pltpu.VMEM((2, COLS, ROWS), BF16),
            pltpu.VMEM((2, 4, PART, ROWS), BF16),
            pltpu.VMEM((4, 8, ROWS), F32),
            pltpu.VMEM((3, 8, 8, 128), F32),
            pltpu.VMEM((3, 8, 8, 128), F32),
            pltpu.VMEM((PART, TOK), F32),
            pltpu.VMEM((PART, TOK), BF16),
            pltpu.VMEM((4, 4, 2, PART, 128), BF16),
            pltpu.VMEM((4, 4, PART, 128), BF16),
            *[pltpu.VMEM((4, PART, 128), BF16)] * 7,
            pltpu.VMEM((1, ROWS), jnp.int32),
            pltpu.SMEM((NSRC,), F32),
            pltpu.VMEM((8, 128), F32),
            pltpu.SemaphoreType.DMA((16,)),
            pltpu.SemaphoreType.DMA((SEND.used,)),
            pltpu.SemaphoreType.DMA((RECV.used,)),
        ],
        compiler_params=pltpu.CompilerParams(
            collective_id=0, has_side_effects=True, vmem_limit_bytes=60 * 2**20
        ),
    )(
        tokens,
        gate_pre,
        up_act,
        hidden_cot,
        source_ids.reshape(1, ROWS),
        data_weight,
        grad,
        moment_m,
        moment_v,
        val_adjoint,
    )
    curvature, source_grad = pl.pallas_call(
        emit,
        name="emit",
        out_shape=(jax.ShapeDtypeStruct((ROWS, COLS), F32), jax.ShapeDtypeStruct((1, NSRC), F32)),
        in_specs=[vmem, vmem],
        out_specs=(vmem, vmem),
        compiler_params=pltpu.CompilerParams(vmem_limit_bytes=60 * 2**20),
    )(turned, sums)
    return curvature, source_grad.reshape(NSRC)


def solution(mesh):
    split = P("dp", "tensor")
    in_specs = (split, split, split, split, P("dp"), P(), split, split, split, split)
    return jax.shard_map(body, mesh=mesh, in_specs=in_specs, out_specs=(split, P()), check_vma=False)
```

```python
import contextlib

import jax
import jax.numpy as jnp
from jax import lax
from jax.experimental import pallas as pl
from jax.experimental.pallas import tpu as pltpu
from jax.sharding import PartitionSpec as P

CLIP_NORM = 1.0
LEARN_RATE = 0.00015
BETA_ONE = 0.9
BETA_TWO = 0.95
ADAM_EPSILON = 1e-08
NORM_EPSILON = 1e-06

MESH = pl.DeviceIdType.MESH
BF16 = jnp.bfloat16
F32 = jnp.float32

ROWS = 128
COLS = 1792
PART = 448
HALF = 224
TOK = 512
TOKENS = 4096
NSRC = 64


def mark(name):
    return contextlib.nullcontext()


class Slots:
    def __init__(self):
        self.used = 0

    def take(self, count):
        first = self.used
        self.used += count
        return first


RECV = Slots()
TZ = RECV.take(7)
TY = RECV.take(8)
TY_AHEAD = RECV.take(1)
TY_RELAY = RECV.take(1)
XZ = RECV.take(4)
XX = RECV.take(12)
XC = RECV.take(1)
AZ = RECV.take(2)
IZ = RECV.take(1)
N1 = RECV.take(3)
CC = RECV.take(16)
RX = RECV.take(24)
RZ = RECV.take(1)
N2 = RECV.take(3)
SEND = Slots()
S_TZ = SEND.take(1)
S_TY = SEND.take(1)
S_X = SEND.take(1)
S_A = SEND.take(2)
S_I = SEND.take(1)
S_N1 = SEND.take(3)
S_CC = SEND.take(1)
S_R = SEND.take(1)
S_Z = SEND.take(1)
S_N2 = SEND.take(3)


def kernel(
    tokens, gate, up, hid, ids, weight, grad, mom, sec, adj,
    res, src_out,
    grad_v, mom_v, sec_v, adj_v, gate_v, up_v, hid_v,
    tok, tang, xb, acts, act, idb, norm1, norm2, proj, mixed, cb, cr, s0, s1, s2, r0, r1, r2, fin,
    ids_v, weight_s, sums, onehot,
    ls, ss, rs,
):
    dp, tn = lax.axis_index("dp"), lax.axis_index("tensor")
    zh, x, c = lax.div(dp, 8), lax.rem(lax.div(dp, 2), 4), lax.rem(dp, 2)
    zl, y = lax.div(tn, 4), lax.rem(tn, 4)
    z = zh * 2 + zl
    way = 1 - 2 * c

    def dev(z_at, x_at, y_at, c_at):
        return (lax.div(z_at, 2) * 8 + x_at * 2 + c_at, lax.rem(z_at, 2) * 4 + y_at)

    def zs(k):
        return lax.rem(z + k * way + 8, 8)

    def xs(k):
        return lax.rem(x + k * way + 4, 4)

    def ys(k):
        return lax.rem(y + k * way + 4, 4)

    def zhs(k):
        return lax.rem(zh + k + 4, 4)

    def at_zh(zh_at):
        return (zh_at * 8 + x * 2 + c, tn)

    x_dev = {k: dev(z, xs(k), y, c) for k in (1, -1)}
    y_dev = {k: dev(z, x, ys(k), c) for k in (1, -1)}
    z_dev = {k: dev(zs(k), x, y, c) for k in (1, -1)}
    core = dev(z, x, y, 1 - c)

    groups = (
        [dev(z, x, lax.rem(y + d, 4), c) for d in range(1, 4)],
        [dev(lax.rem(z + d, 8), x, y, c) for d in range(1, 8)],
        [dev(z, lax.div(lax.rem(x * 2 + c + d, 8), 2), y, lax.rem(c + d, 2)) for d in range(1, 8)],
    )
    places = (y, z, x * 2 + c)

    def push(src, dst, send, recv, to):
        pltpu.make_async_remote_copy(
            src_ref=src, dst_ref=dst, send_sem=ss.at[send], recv_sem=rs.at[recv], device_id=to, device_id_type=MESH
        ).start()

    def counted(ref, send, recv):
        return pltpu.make_async_remote_copy(
            src_ref=ref, dst_ref=ref, send_sem=ss.at[send], recv_sem=rs.at[recv], device_id=core, device_id_type=MESH
        )

    def arrived(ref, recv):
        counted(ref, 0, recv).wait_recv()

    def drained(ref, send):
        counted(ref, send, 0).wait_send()

    local = []

    def fetch(src, dst):
        copy = pltpu.make_async_copy(src, dst, ls.at[len(local)])
        copy.start()
        local.append(copy)
        return copy

    def shard(z_at, y_at):
        block = lax.rem(z_at, 2) * 4 + y_at
        return tok.at[pl.ds(2 * block, 2), pl.ds(pl.multiple_of(lax.div(z_at, 2) * ROWS, ROWS), ROWS), :]

    def spread(buf, send, recv, stage, value):
        place = places[stage]
        buf[stage, place] = value
        for to in groups[stage]:
            push(buf.at[stage, place], buf.at[stage, place], send + stage, recv + stage, to)

    def collect(buf, recv, stage):
        size = len(groups[stage]) + 1
        arrived(buf.at[stage, pl.ds(0, size - 1)], recv + stage)
        total = buf[stage, 0]
        for k in range(1, size):
            total = total + buf[stage, k]
        return total

    get_grad = fetch(grad, grad_v)
    with mark("barrier"):
        barrier = pltpu.get_barrier_semaphore()
        for group in (groups[1], groups[0], groups[2]):
            for to in group:
                pl.semaphore_signal(barrier, inc=1, device_id=to, device_id_type=MESH)
    block = zl * 4 + y
    own_rows = pl.ds(pl.multiple_of(zh * ROWS, ROWS), ROWS)
    get_tok = [fetch(tokens.at[:, pl.ds(h * 256, 256)], tok.at[2 * block + h, own_rows, :]) for h in range(2)]
    get_acts = [fetch(gate, gate_v), fetch(up, up_v), fetch(hid, hid_v), fetch(ids, ids_v), fetch(weight, weight_s)]
    get_rest = [fetch(mom, mom_v), fetch(sec, sec_v), fetch(adj, adj_v)]
    with mark("barrier_wait"):
        pl.semaphore_wait(barrier, sum(len(group) for group in groups))

    get_grad.wait()

    def square(k, total):
        part = grad_v[pl.ds(pl.multiple_of(k * 8, 8), 8), :]
        part = part * part
        for j in range(COLS // 128):
            total = total + part[:, j * 128 : (j + 1) * 128]
        return total

    with mark("squares"):
        spread(norm1, S_N1, N1, 0, lax.fori_loop(0, ROWS // 8, square, jnp.zeros((8, 128), F32)))

    for copy in get_tok:
        copy.wait()

    def pass_y(m, z_at):
        here = shard(z_at, y)
        push(here, here, S_TY, TY + m, y_dev[1])
        push(here, here, S_TY, TY_AHEAD, y_dev[-1])

    def relay_y(m, z_at):
        with mark(f"ry{m}"):
            there = shard(z_at, ys(-1))
            arrived(there, TY + m)
            push(there, there, S_TY, TY_RELAY, y_dev[1])

    own = shard(z, y)
    push(own, own, S_TZ, TZ, z_dev[1])
    push(own, own, S_TZ, TZ + 4, z_dev[-1])
    pass_y(0, z)

    for copy in get_acts:
        copy.wait()
    ids_row = ids_v[...]
    weight_row = jnp.zeros((1, ROWS), F32)
    for k in range(NSRC):
        weight_row = jnp.where(ids_row == k, weight_s[k], weight_row)
    weight_row = weight_row / TOKENS
    weight_col = jnp.broadcast_to(weight_row, (ROWS, ROWS)).T
    idb[zh] = jnp.broadcast_to(ids_row.astype(F32), (8, ROWS))

    def activation(j, carry):
        cols = pl.ds(pl.multiple_of(j * 128, 128), 128)
        pre = gate_v[:, cols].astype(F32)
        sigma = 1.0 / (1.0 + jnp.exp(-pre))
        coupling = up_v[:, cols].astype(F32) * hid_v[:, cols].astype(F32)
        first = coupling * sigma * (1.0 + pre * (1.0 - sigma))
        second = coupling * sigma * (1.0 - sigma) * (2.0 + pre * (1.0 - 2.0 * sigma))
        acts[0, cols, :] = first.astype(BF16).T
        acts[1, cols, :] = (second * weight_col).astype(BF16).T
        return carry

    with mark("activation"):
        lax.fori_loop(0, COLS // 128, activation, 0)

    def part_rows(q):
        return pl.ds(pl.multiple_of(q * PART, 64), PART)

    def share_acts(which):
        for d in (2, 1, 3):
            push(acts.at[which, part_rows(zhs(d)), :], act.at[which, zh], S_A + which, AZ + which, at_zh(zhs(d)))

    for d in (1, 2, 3):
        push(idb.at[zh], idb.at[zh], S_I, IZ, at_zh(zhs(d)))
    keep_act = [fetch(acts.at[k, part_rows(zh), :], act.at[k, zh]) for k in range(2)]

    def forward_z(k):
        with mark(f"fz{k}"):
            z_at = zs(-k)
            arrived(shard(z_at, y), TZ + k - 1)
            if k < 4:
                push(shard(z_at, y), shard(z_at, y), S_TZ, TZ + k, z_dev[1])
            pass_y(2 * k - 1, z_at)

    def backward_z(k):
        with mark(f"bz{k}"):
            z_at = zs(k)
            arrived(shard(z_at, y), TZ + 4 + k - 1)
            if k < 3:
                push(shard(z_at, y), shard(z_at, y), S_TZ, TZ + 4 + k, z_dev[-1])
            pass_y(2 * k, z_at)

    with mark("norm_a"):
        spread(norm1, S_N1, N1, 1, collect(norm1, N1, 0))
    forward_z(1)
    backward_z(1)
    with mark("norm_b"):
        spread(norm1, S_N1, N1, 2, collect(norm1, N1, 1))
    relay_y(0, z)
    forward_z(2)
    backward_z(2)
    with mark("norm_c"):
        total_sq = jnp.sum(collect(norm1, N1, 2), keepdims=True) + NORM_EPSILON
    clip = jnp.minimum(CLIP_NORM * lax.rsqrt(total_sq), 1.0)
    for copy in get_rest:
        copy.wait()

    def tangent(q):
        first = lax.div(7 * q, 2)

        def tile(j, carry):
            cols = pl.ds(pl.multiple_of((first + j) * 128, 128), 128)
            clipped = clip * grad_v[:, cols]
            moment_new = BETA_ONE * mom_v[:, cols] + (1.0 - BETA_ONE) * clipped
            second_new = BETA_TWO * sec_v[:, cols] + (1.0 - BETA_TWO) * clipped * clipped
            root_v = jnp.sqrt(second_new)
            inverse = 1.0 / (root_v + ADAM_EPSILON)
            jacobian = -LEARN_RATE * (
                (1.0 - BETA_ONE) * inverse - moment_new * (1.0 - BETA_TWO) * clipped * (inverse * inverse / root_v)
            )
            pulled = jacobian * adj_v[:, cols]
            tang[q, pl.ds(pl.multiple_of(j * 128, 128), 128), :] = (clip * pulled).astype(BF16).T
            return carry

        lax.fori_loop(0, 4, tile, 0)
        return tang.at[q, pl.ds(pl.multiple_of(lax.rem(q, 2) * 64, 64), PART), :]

    def x_first(d):
        with mark(f"tangent{d}"):
            push(tangent(zhs(d)), xb.at[dp], S_X, XZ + d, at_zh(zhs(d)))

    x_first(1)
    x_first(3)
    x_first(2)
    with mark("tangent0"):
        keep = fetch(tangent(zh), xb.at[dp])
    relay_y(1, zs(-1))
    relay_y(2, zs(1))

    def x_block(x_at, d):
        return xb.at[zhs(-d) * 8 + x_at * 2 + c]

    def x_own(d):
        with mark(f"xown{d}"):
            here = x_block(x, d)
            if d:
                arrived(here, XZ + d)
            else:
                keep.wait()
            push(here, here, S_X, XX + d, x_dev[1])
            push(here, here, S_X, XX + 4 + d, x_dev[-1])
            push(here, here, S_X, XC, core)

    def x_sides(d):
        with mark(f"xside{d}"):
            there = x_block(xs(-1), d)
            arrived(there, XX + d)
            push(there, there, S_X, XX + 8 + d, x_dev[1])
            push(there, there, S_X, XC, core)
            there = x_block(xs(1), d)
            arrived(there, XX + 4 + d)
            push(there, there, S_X, XC, core)

    def x_relay(d):
        with mark(f"xrelay{d}"):
            there = x_block(xs(2), d)
            arrived(there, XX + 8 + d)
            push(there, there, S_X, XC, core)

    x_own(0)
    forward_z(3)
    backward_z(3)
    x_sides(0)
    x_own(1)
    x_own(3)
    share_acts(1)
    relay_y(3, zs(-2))
    relay_y(4, zs(2))
    x_relay(0)
    x_own(2)
    x_sides(1)
    x_sides(3)
    forward_z(4)
    relay_y(5, zs(-3))
    relay_y(6, zs(3))
    x_sides(2)
    x_relay(1)
    x_relay(3)
    relay_y(7, zs(-4))
    share_acts(0)
    arrived(idb.at[pl.ds(0, 3)], IZ)
    source = lax.broadcasted_iota(jnp.int32, (128, ROWS), 0).astype(F32)
    for k in range(4):
        onehot[:, k * ROWS : (k + 1) * ROWS] = (source == idb[k, 0:1, :]).astype(F32)
    x_relay(2)

    def first_product(places):
        blocks = [k for y_at in places for k in (y_at, y_at + 4)]
        left = jnp.concatenate([xb[4 * k + i] for k in blocks for i in range(4)], axis=1)
        right = jnp.concatenate([tok[2 * k + i] for k in blocks for i in range(2)], axis=1)
        return lax.dot_general(left, right, (((1,), (1,)), ((), ())), preferred_element_type=F32)

    with mark("ynear"):
        arrived(tok.at[pl.ds(0, 4)], TY_AHEAD)
    with mark("xcore"):
        arrived(xb.at[pl.ds(0, 16)], XC)
    with mark("product1"):
        proj[...] = first_product([y, ys(-1), ys(1)])
    with mark("yfar"):
        arrived(tok.at[pl.ds(0, 4)], TY_RELAY)
    with mark("product1b"):
        proj[...] += first_product([ys(2)])

    with mark("second_wait"):
        for copy in keep_act:
            copy.wait()
        arrived(act.at[1, pl.ds(0, 3)], AZ + 1)

    with mark("mix"):
        for k in range(4):
            cols = pl.ds(k * ROWS, ROWS)
            mixed[:, cols] = (proj[:, cols] * act[1, k].astype(F32)).astype(BF16)

    def source_sums():
        arrived(act.at[0, pl.ds(0, 3)], AZ)
        per_tok = [
            jnp.sum(proj[:, pl.ds(k * ROWS, ROWS)] * act[0, k].astype(F32), axis=0, keepdims=True) for k in range(4)
        ]
        return lax.dot_general(
            jnp.broadcast_to(jnp.concatenate(per_tok, axis=1), (8, TOK)),
            onehot[...],
            (((1,), (1,)), ((), ())),
            precision=lax.Precision.HIGHEST,
            preferred_element_type=F32,
        )

    order = (2, 1, 3, 0)
    behind, ahead = 3 - 2 * c, 1 + 2 * c

    def pair_product(j):
        zh_at = zhs(order[j])
        at = [lax.rem(x + offset, 4) for offset in (1, 3)]
        right = jnp.concatenate([tok[zh_at * 4 + x_at] for x_at in at], axis=1)
        whole = jnp.dot(mixed[...], right, preferred_element_type=F32)
        for k, x_at in enumerate(at):
            for half_at in range(2):
                cols = slice(256 * k + 128 * half_at, 256 * k + 128 * half_at + 128)
                cb[x_at, zh_at, half_at] = whole[:, cols].astype(BF16)
            push(cb.at[x_at, zh_at, 1 - c], cr.at[x_at, zh_at], S_CC, CC + (1 + 2 * k) * 4 + j, core)

    def second_product(offset, j):
        x_at, zh_at = lax.rem(x + offset, 4), zhs(order[j])
        whole = jnp.dot(mixed[...], tok[zh_at * 4 + x_at], preferred_element_type=F32)
        cb[x_at, zh_at, 0] = whole[:, :128].astype(BF16)
        cb[x_at, zh_at, 1] = whole[:, 128:].astype(BF16)
        push(cb.at[x_at, zh_at, 1 - c], cr.at[x_at, zh_at], S_CC, CC + offset * 4 + j, core)

    def half(h):
        return pl.ds(h * HALF, HALF)

    def both(offset, j, h):
        x_at, zh_at = lax.rem(x + offset, 4), zhs(order[j])
        if h == 0:
            arrived(cr.at[x_at, zh_at], CC + offset * 4 + j)
        return cb[x_at, zh_at, c, half(h)].astype(F32) + cr[x_at, zh_at, half(h)].astype(F32)

    def opposite(j, h):
        with mark(f"opposite{j}{h}"):
            s0[j, half(h)] = both(2, j, h).astype(BF16)
            push(s0.at[j, half(h)], r0.at[j, half(h)], S_R, RX + 2 * j + h, x_dev[1])

    def backward(j, h):
        with mark(f"backward{j}{h}"):
            s2[j, half(h)] = both(behind, j, h).astype(BF16)
            push(s2.at[j, half(h)], r2.at[j, half(h)], S_R, RX + 16 + 2 * j + h, x_dev[-1])

    def onward(j, h):
        with mark(f"onward{j}{h}"):
            part = both(ahead, j, h)
            arrived(r0.at[j, half(h)], RX + 2 * j + h)
            s1[j, half(h)] = (part + r0[j, half(h)].astype(F32)).astype(BF16)
            push(s1.at[j, half(h)], r1.at[j, half(h)], S_R, RX + 8 + 2 * j + h, x_dev[1])

    def finish(j, h):
        with mark(f"finish{j}{h}"):
            part = both(0, j, h)
            arrived(r2.at[j, half(h)], RX + 16 + 2 * j + h)
            part = part + r2[j, half(h)].astype(F32)
            arrived(r1.at[j, half(h)], RX + 8 + 2 * j + h)
            fin[j, half(h)] = (part + r1[j, half(h)].astype(F32)).astype(BF16)
            d = order[j]
            rows = pl.ds(pl.multiple_of(zh * PART + h * HALF, 32), HALF)
            if d:
                push(fin.at[j, half(h)], res.at[rows, :], S_Z, RZ, at_zh(zhs(d)))
            elif h:
                fetch(fin.at[j], res.at[part_rows(zh), :])

    todo = (
        (2, 0), (1, 0), (3, 0), (2, 1), (1, 1), (3, 1), (2, 2), (1, 2), (3, 2), (0, 0), (2, 3), (1, 3), (3, 3), (0, 1), (0, 2), (0, 3),
    )
    then = {
        4: [(opposite, 0, 0), (opposite, 0, 1)],
        6: [(backward, 0, 0), (backward, 0, 1)],
        8: [(opposite, 1, 0)],
        9: [(backward, 1, 0)],
        11: [(onward, 0, 0), (onward, 0, 1)],
        12: [(opposite, 2, 0), (backward, 2, 0)],
        13: [(opposite, 1, 1), (backward, 1, 1)],
        15: [(onward, 1, 0), (opposite, 2, 1), (backward, 2, 1)],
    }
    for i, (offset, j) in enumerate(todo):
        with mark(f"second{i}"):
            if offset == 1:
                pair_product(j)
            elif offset != 3:
                second_product(offset, j)
        for step, at, h in then.get(i, ()):
            step(at, h)
    with mark("n2_0"):
        spread(norm2, S_N2, N2, 1, source_sums())
    finish(0, 0)
    finish(0, 1)
    onward(2, 0)
    onward(1, 1)
    opposite(3, 0)
    backward(3, 0)
    finish(1, 0)
    with mark("n2_1"):
        spread(norm2, S_N2, N2, 0, collect(norm2, N2, 1))
    onward(2, 1)
    opposite(3, 1)
    backward(3, 1)
    finish(2, 0)
    finish(1, 1)
    with mark("n2_2"):
        spread(norm2, S_N2, N2, 2, collect(norm2, N2, 0))
    onward(3, 0)
    finish(2, 1)
    onward(3, 1)
    finish(3, 0)
    finish(3, 1)
    with mark("n2_3"):
        sums[...] = collect(norm2, N2, 2) / TOKENS
        fetch(sums, src_out)
    with mark("zlast"):
        arrived(cr.at[0, pl.ds(0, 3)], RZ)
    with mark("drain"):
        local[-1].wait()
        local[-2].wait()
        drained(tok.at[pl.ds(0, 7), pl.ds(0, 256)], S_TZ)
        drained(tok.at[pl.ds(0, 12)], S_TY)
        drained(xb.at[pl.ds(0, 31)], S_X)
        for which in range(2):
            drained(act.at[which, pl.ds(0, 3)], S_A + which)
        drained(idb.at[pl.ds(0, 3)], S_I)
        drained(cr, S_CC)
        drained(cr.at[pl.ds(0, 3)], S_R)
        drained(cr.at[0, pl.ds(0, 3)], S_Z)
        for stage in range(3):
            drained(norm1.at[0, pl.ds(0, len(groups[stage]))], S_N1 + stage)
            drained(norm2.at[0, pl.ds(0, len(groups[stage]))], S_N2 + stage)


def emit(res, sums, out, src):
    def turn(j, carry):
        cols = pl.ds(pl.multiple_of(j * 128, 128), 128)
        out[:, cols] = res[cols, :].T.astype(F32)
        return carry

    lax.fori_loop(0, COLS // 128, turn, 0, unroll=14)
    src[...] = sums[0:1, :NSRC]


def body(tokens, gate_pre, up_act, hidden_cot, source_ids, data_weight, grad, moment_m, moment_v, val_adjoint):
    hbm = pl.BlockSpec(memory_space=pl.ANY)
    vmem = pl.BlockSpec(memory_space=pltpu.VMEM)
    turned, sums = pl.pallas_call(
        kernel,
        name="metagradient",
        out_shape=(jax.ShapeDtypeStruct((COLS, ROWS), BF16), jax.ShapeDtypeStruct((8, 128), F32)),
        in_specs=[hbm] * 10,
        out_specs=(hbm, hbm),
        scratch_shapes=[
            *[pltpu.VMEM((ROWS, COLS), F32)] * 4,
            *[pltpu.VMEM((ROWS, COLS), BF16)] * 3,
            pltpu.VMEM((16, TOK, 256), BF16),
            pltpu.VMEM((4, 512, ROWS), BF16),
            pltpu.VMEM((32, PART, 128), BF16),
            pltpu.VMEM((2, COLS, ROWS), BF16),
            pltpu.VMEM((2, 4, PART, ROWS), BF16),
            pltpu.VMEM((4, 8, ROWS), F32),
            pltpu.VMEM((3, 8, 8, 128), F32),
            pltpu.VMEM((3, 8, 8, 128), F32),
            pltpu.VMEM((PART, TOK), F32),
            pltpu.VMEM((PART, TOK), BF16),
            pltpu.VMEM((4, 4, 2, PART, 128), BF16),
            pltpu.VMEM((4, 4, PART, 128), BF16),
            *[pltpu.VMEM((4, PART, 128), BF16)] * 7,
            pltpu.VMEM((1, ROWS), jnp.int32),
            pltpu.SMEM((NSRC,), F32),
            pltpu.VMEM((8, 128), F32),
            pltpu.VMEM((128, TOK), F32),
            pltpu.SemaphoreType.DMA((16,)),
            pltpu.SemaphoreType.DMA((SEND.used,)),
            pltpu.SemaphoreType.DMA((RECV.used,)),
        ],
        compiler_params=pltpu.CompilerParams(
            collective_id=0, has_side_effects=True, vmem_limit_bytes=60 * 2**20
        ),
    )(
        tokens,
        gate_pre,
        up_act,
        hidden_cot,
        source_ids.reshape(1, ROWS),
        data_weight,
        grad,
        moment_m,
        moment_v,
        val_adjoint,
    )
    curvature, source_grad = pl.pallas_call(
        emit,
        name="emit",
        out_shape=(jax.ShapeDtypeStruct((ROWS, COLS), F32), jax.ShapeDtypeStruct((1, NSRC), F32)),
        in_specs=[vmem, vmem],
        out_specs=(vmem, vmem),
        compiler_params=pltpu.CompilerParams(vmem_limit_bytes=60 * 2**20),
    )(turned, sums)
    return curvature, source_grad.reshape(NSRC)


def solution(mesh):
    split = P("dp", "tensor")
    in_specs = (split, split, split, split, P("dp"), P(), split, split, split, split)
    return jax.shard_map(body, mesh=mesh, in_specs=in_specs, out_specs=(split, P()), check_vma=False)
```

```python
import contextlib

import jax
import jax.numpy as jnp
from jax import lax
from jax.experimental import pallas as pl
from jax.experimental.pallas import tpu as pltpu
from jax.sharding import PartitionSpec as P

CLIP_NORM = 1.0
LEARN_RATE = 0.00015
BETA_ONE = 0.9
BETA_TWO = 0.95
ADAM_EPSILON = 1e-08
NORM_EPSILON = 1e-06

MESH = pl.DeviceIdType.MESH
BF16 = jnp.bfloat16
F32 = jnp.float32

ROWS = 128
COLS = 1792
PART = 448
HALF = 224
TOK = 512
TOKENS = 4096
NSRC = 64


def mark(name):
    return contextlib.nullcontext()


class Slots:
    def __init__(self):
        self.used = 0

    def take(self, count):
        first = self.used
        self.used += count
        return first


RECV = Slots()
TZ = RECV.take(7)
TY = RECV.take(8)
TY_AHEAD = RECV.take(1)
TY_RELAY = RECV.take(1)
XZ = RECV.take(4)
XX = RECV.take(12)
XC = RECV.take(1)
AZ = RECV.take(2)
IZ = RECV.take(1)
N1 = RECV.take(3)
CC = RECV.take(16)
RX = RECV.take(24)
RZ = RECV.take(1)
N2 = RECV.take(3)
SEND = Slots()
S_TZ = SEND.take(1)
S_TY = SEND.take(1)
S_X = SEND.take(1)
S_A = SEND.take(2)
S_I = SEND.take(1)
S_N1 = SEND.take(3)
S_CC = SEND.take(1)
S_R = SEND.take(1)
S_Z = SEND.take(1)
S_N2 = SEND.take(3)


def kernel(
    tokens, gate, up, hid, ids, weight, grad, mom, sec, adj,
    res, src_out,
    grad_v, mom_v, sec_v, adj_v, gate_v, up_v, hid_v,
    tok, tang, xb, acts, act, idb, norm1, norm2, proj, mixed, cb, cr, s0, s1, s2, r0, r1, r2, fin,
    ids_v, weight_s, sums, onehot,
    ls, ss, rs,
):
    dp, tn = lax.axis_index("dp"), lax.axis_index("tensor")
    zh, x, c = lax.div(dp, 8), lax.rem(lax.div(dp, 2), 4), lax.rem(dp, 2)
    zl, y = lax.div(tn, 4), lax.rem(tn, 4)
    z = zh * 2 + zl
    way = 1 - 2 * c

    def dev(z_at, x_at, y_at, c_at):
        return (lax.div(z_at, 2) * 8 + x_at * 2 + c_at, lax.rem(z_at, 2) * 4 + y_at)

    def zs(k):
        return lax.rem(z + k * way + 8, 8)

    def xs(k):
        return lax.rem(x + k * way + 4, 4)

    def ys(k):
        return lax.rem(y + k * way + 4, 4)

    def zhs(k):
        return lax.rem(zh + k + 4, 4)

    def at_zh(zh_at):
        return (zh_at * 8 + x * 2 + c, tn)

    x_dev = {k: dev(z, xs(k), y, c) for k in (1, -1)}
    y_dev = {k: dev(z, x, ys(k), c) for k in (1, -1)}
    z_dev = {k: dev(zs(k), x, y, c) for k in (1, -1)}
    core = dev(z, x, y, 1 - c)

    groups = (
        [dev(z, x, lax.rem(y + d, 4), c) for d in range(1, 4)],
        [dev(lax.rem(z + d, 8), x, y, c) for d in range(1, 8)],
        [dev(z, lax.div(lax.rem(x * 2 + c + d, 8), 2), y, lax.rem(c + d, 2)) for d in range(1, 8)],
    )
    places = (y, z, x * 2 + c)

    def push(src, dst, send, recv, to):
        pltpu.make_async_remote_copy(
            src_ref=src, dst_ref=dst, send_sem=ss.at[send], recv_sem=rs.at[recv], device_id=to, device_id_type=MESH
        ).start()

    def counted(ref, send, recv):
        return pltpu.make_async_remote_copy(
            src_ref=ref, dst_ref=ref, send_sem=ss.at[send], recv_sem=rs.at[recv], device_id=core, device_id_type=MESH
        )

    def arrived(ref, recv):
        counted(ref, 0, recv).wait_recv()

    def drained(ref, send):
        counted(ref, send, 0).wait_send()

    local = []

    def fetch(src, dst):
        copy = pltpu.make_async_copy(src, dst, ls.at[len(local)])
        copy.start()
        local.append(copy)
        return copy

    def shard(z_at, y_at):
        block = lax.rem(z_at, 2) * 4 + y_at
        return tok.at[pl.ds(2 * block, 2), pl.ds(pl.multiple_of(lax.div(z_at, 2) * ROWS, ROWS), ROWS), :]

    def spread(buf, send, recv, stage, value):
        place = places[stage]
        buf[stage, place] = value
        for to in groups[stage]:
            push(buf.at[stage, place], buf.at[stage, place], send + stage, recv + stage, to)

    def collect(buf, recv, stage):
        size = len(groups[stage]) + 1
        arrived(buf.at[stage, pl.ds(0, size - 1)], recv + stage)
        total = buf[stage, 0]
        for k in range(1, size):
            total = total + buf[stage, k]
        return total

    get_grad = fetch(grad, grad_v)
    with mark("barrier"):
        barrier = pltpu.get_barrier_semaphore()
        for group in (groups[1], groups[0], groups[2]):
            for to in group:
                pl.semaphore_signal(barrier, inc=1, device_id=to, device_id_type=MESH)
    block = zl * 4 + y
    own_rows = pl.ds(pl.multiple_of(zh * ROWS, ROWS), ROWS)
    get_tok = [fetch(tokens.at[:, pl.ds(h * 256, 256)], tok.at[2 * block + h, own_rows, :]) for h in range(2)]
    get_acts = [fetch(gate, gate_v), fetch(up, up_v), fetch(hid, hid_v), fetch(ids, ids_v), fetch(weight, weight_s)]
    get_rest = [fetch(mom, mom_v), fetch(sec, sec_v), fetch(adj, adj_v)]
    with mark("barrier_wait"):
        pl.semaphore_wait(barrier, sum(len(group) for group in groups))

    get_grad.wait()

    def square(k, total):
        part = grad_v[pl.ds(pl.multiple_of(k * 8, 8), 8), :]
        part = part * part
        for j in range(COLS // 128):
            total = total + part[:, j * 128 : (j + 1) * 128]
        return total

    with mark("squares"):
        spread(norm1, S_N1, N1, 0, lax.fori_loop(0, ROWS // 8, square, jnp.zeros((8, 128), F32)))

    for copy in get_tok:
        copy.wait()

    def pass_y(m, z_at):
        here = shard(z_at, y)
        push(here, here, S_TY, TY + m, y_dev[1])
        push(here, here, S_TY, TY_AHEAD, y_dev[-1])

    def relay_y(m, z_at):
        with mark(f"ry{m}"):
            there = shard(z_at, ys(-1))
            arrived(there, TY + m)
            push(there, there, S_TY, TY_RELAY, y_dev[1])

    own = shard(z, y)
    push(own, own, S_TZ, TZ, z_dev[1])
    push(own, own, S_TZ, TZ + 4, z_dev[-1])
    pass_y(0, z)

    for copy in get_acts:
        copy.wait()
    ids_row = ids_v[...]
    weight_row = jnp.zeros((1, ROWS), F32)
    for k in range(NSRC):
        weight_row = jnp.where(ids_row == k, weight_s[k], weight_row)
    weight_row = weight_row / TOKENS
    weight_col = jnp.broadcast_to(weight_row, (ROWS, ROWS)).T
    idb[zh] = jnp.broadcast_to(ids_row.astype(F32), (8, ROWS))

    def activation(j, carry):
        cols = pl.ds(pl.multiple_of(j * 128, 128), 128)
        pre = gate_v[:, cols].astype(F32)
        sigma = 1.0 / (1.0 + jnp.exp(-pre))
        coupling = up_v[:, cols].astype(F32) * hid_v[:, cols].astype(F32)
        first = coupling * sigma * (1.0 + pre * (1.0 - sigma))
        second = coupling * sigma * (1.0 - sigma) * (2.0 + pre * (1.0 - 2.0 * sigma))
        acts[0, cols, :] = first.astype(BF16).T
        acts[1, cols, :] = (second * weight_col).astype(BF16).T
        return carry

    with mark("activation"):
        lax.fori_loop(0, COLS // 128, activation, 0)

    def part_rows(q):
        return pl.ds(pl.multiple_of(q * PART, 64), PART)

    def share_acts(which, partners=(1, 3, 2)):
        for d in partners:
            push(acts.at[which, part_rows(zhs(d)), :], act.at[which, zh], S_A + which, AZ + which, at_zh(zhs(d)))

    for d in (1, 2, 3):
        push(idb.at[zh], idb.at[zh], S_I, IZ, at_zh(zhs(d)))
    keep_act = [fetch(acts.at[k, part_rows(zh), :], act.at[k, zh]) for k in range(2)]

    def forward_z(k):
        with mark(f"fz{k}"):
            z_at = zs(-k)
            arrived(shard(z_at, y), TZ + k - 1)
            if k < 4:
                push(shard(z_at, y), shard(z_at, y), S_TZ, TZ + k, z_dev[1])
            pass_y(2 * k - 1, z_at)

    def backward_z(k):
        with mark(f"bz{k}"):
            z_at = zs(k)
            arrived(shard(z_at, y), TZ + 4 + k - 1)
            if k < 3:
                push(shard(z_at, y), shard(z_at, y), S_TZ, TZ + 4 + k, z_dev[-1])
            pass_y(2 * k, z_at)

    with mark("norm_a"):
        spread(norm1, S_N1, N1, 1, collect(norm1, N1, 0))
    forward_z(1)
    backward_z(1)
    with mark("norm_b"):
        spread(norm1, S_N1, N1, 2, collect(norm1, N1, 1))
    relay_y(0, z)
    forward_z(2)
    backward_z(2)
    with mark("norm_c"):
        total_sq = jnp.sum(collect(norm1, N1, 2), keepdims=True) + NORM_EPSILON
    clip = jnp.minimum(CLIP_NORM * lax.rsqrt(total_sq), 1.0)
    for copy in get_rest:
        copy.wait()

    def tangent(q):
        first = lax.div(7 * q, 2)

        def tile(j, carry):
            cols = pl.ds(pl.multiple_of((first + j) * 128, 128), 128)
            clipped = clip * grad_v[:, cols]
            moment_new = BETA_ONE * mom_v[:, cols] + (1.0 - BETA_ONE) * clipped
            second_new = BETA_TWO * sec_v[:, cols] + (1.0 - BETA_TWO) * clipped * clipped
            root_v = jnp.sqrt(second_new)
            inverse = 1.0 / (root_v + ADAM_EPSILON)
            jacobian = -LEARN_RATE * (
                (1.0 - BETA_ONE) * inverse - moment_new * (1.0 - BETA_TWO) * clipped * (inverse * inverse / root_v)
            )
            pulled = jacobian * adj_v[:, cols]
            tang[q, pl.ds(pl.multiple_of(j * 128, 128), 128), :] = (clip * pulled).astype(BF16).T
            return carry

        lax.fori_loop(0, 4, tile, 0)
        return tang.at[q, pl.ds(pl.multiple_of(lax.rem(q, 2) * 64, 64), PART), :]

    def x_first(d):
        with mark(f"tangent{d}"):
            push(tangent(zhs(d)), xb.at[dp], S_X, XZ + d, at_zh(zhs(d)))

    x_first(1)
    x_first(3)
    x_first(2)
    with mark("tangent0"):
        keep = fetch(tangent(zh), xb.at[dp])
    relay_y(1, zs(-1))
    relay_y(2, zs(1))

    def x_block(x_at, d):
        return xb.at[zhs(-d) * 8 + x_at * 2 + c]

    def x_own(d):
        with mark(f"xown{d}"):
            here = x_block(x, d)
            if d:
                arrived(here, XZ + d)
            else:
                keep.wait()
            push(here, here, S_X, XX + d, x_dev[1])
            push(here, here, S_X, XX + 4 + d, x_dev[-1])
            push(here, here, S_X, XC, core)

    def x_sides(d):
        with mark(f"xside{d}"):
            there = x_block(xs(-1), d)
            arrived(there, XX + d)
            push(there, there, S_X, XX + 8 + d, x_dev[1])
            push(there, there, S_X, XC, core)
            there = x_block(xs(1), d)
            arrived(there, XX + 4 + d)
            push(there, there, S_X, XC, core)

    def x_relay(d):
        with mark(f"xrelay{d}"):
            there = x_block(xs(2), d)
            arrived(there, XX + 8 + d)
            push(there, there, S_X, XC, core)

    x_own(0)
    forward_z(3)
    backward_z(3)
    x_sides(0)
    x_own(1)
    x_own(3)
    share_acts(1, (1, 3))
    relay_y(3, zs(-2))
    relay_y(4, zs(2))
    x_relay(0)
    x_own(2)
    share_acts(1, (2,))
    x_sides(1)
    x_sides(3)
    forward_z(4)
    relay_y(5, zs(-3))
    relay_y(6, zs(3))
    x_sides(2)
    x_relay(1)
    x_relay(3)
    relay_y(7, zs(-4))
    share_acts(0)
    arrived(idb.at[pl.ds(0, 3)], IZ)
    source = lax.broadcasted_iota(jnp.int32, (128, ROWS), 0).astype(F32)
    for k in range(4):
        onehot[:, k * ROWS : (k + 1) * ROWS] = (source == idb[k, 0:1, :]).astype(F32)
    x_relay(2)

    def first_product(places):
        blocks = [k for y_at in places for k in (y_at, y_at + 4)]
        left = jnp.concatenate([xb[4 * k + i] for k in blocks for i in range(4)], axis=1)
        right = jnp.concatenate([tok[2 * k + i] for k in blocks for i in range(2)], axis=1)
        return lax.dot_general(left, right, (((1,), (1,)), ((), ())), preferred_element_type=F32)

    with mark("ynear"):
        arrived(tok.at[pl.ds(0, 4)], TY_AHEAD)
    with mark("xcore"):
        arrived(xb.at[pl.ds(0, 16)], XC)
    with mark("product1"):
        proj[...] = first_product([y, ys(-1), ys(1)])
    with mark("yfar"):
        arrived(tok.at[pl.ds(0, 4)], TY_RELAY)
    with mark("product1b"):
        proj[...] += first_product([ys(2)])

    with mark("second_wait"):
        for copy in keep_act:
            copy.wait()
        arrived(act.at[1, pl.ds(0, 3)], AZ + 1)

    with mark("mix"):
        for k in range(4):
            cols = pl.ds(k * ROWS, ROWS)
            mixed[:, cols] = (proj[:, cols] * act[1, k].astype(F32)).astype(BF16)

    def source_sums():
        arrived(act.at[0, pl.ds(0, 3)], AZ)
        per_tok = [
            jnp.sum(proj[:, pl.ds(k * ROWS, ROWS)] * act[0, k].astype(F32), axis=0, keepdims=True) for k in range(4)
        ]
        return lax.dot_general(
            jnp.broadcast_to(jnp.concatenate(per_tok, axis=1), (8, TOK)),
            onehot[...],
            (((1,), (1,)), ((), ())),
            precision=lax.Precision.HIGHEST,
            preferred_element_type=F32,
        )

    order = (2, 1, 3, 0)
    behind, ahead = 3 - 2 * c, 1 + 2 * c

    def pair_product(j):
        zh_at = zhs(order[j])
        at = [lax.rem(x + offset, 4) for offset in (1, 3)]
        right = jnp.concatenate([tok[zh_at * 4 + x_at] for x_at in at], axis=1)
        whole = jnp.dot(mixed[...], right, preferred_element_type=F32)
        for k, x_at in enumerate(at):
            for half_at in range(2):
                cols = slice(256 * k + 128 * half_at, 256 * k + 128 * half_at + 128)
                cb[x_at, zh_at, half_at] = whole[:, cols].astype(BF16)
            push(cb.at[x_at, zh_at, 1 - c], cr.at[x_at, zh_at], S_CC, CC + (1 + 2 * k) * 4 + j, core)

    def second_product(offset, j):
        x_at, zh_at = lax.rem(x + offset, 4), zhs(order[j])
        whole = jnp.dot(mixed[...], tok[zh_at * 4 + x_at], preferred_element_type=F32)
        cb[x_at, zh_at, 0] = whole[:, :128].astype(BF16)
        cb[x_at, zh_at, 1] = whole[:, 128:].astype(BF16)
        push(cb.at[x_at, zh_at, 1 - c], cr.at[x_at, zh_at], S_CC, CC + offset * 4 + j, core)

    def half(h):
        return pl.ds(h * HALF, HALF)

    def both(offset, j, h):
        x_at, zh_at = lax.rem(x + offset, 4), zhs(order[j])
        if h == 0:
            arrived(cr.at[x_at, zh_at], CC + offset * 4 + j)
        return cb[x_at, zh_at, c, half(h)].astype(F32) + cr[x_at, zh_at, half(h)].astype(F32)

    def opposite(j, h):
        with mark(f"opposite{j}{h}"):
            s0[j, half(h)] = both(2, j, h).astype(BF16)
            push(s0.at[j, half(h)], r0.at[j, half(h)], S_R, RX + 2 * j + h, x_dev[1])

    def backward(j, h):
        with mark(f"backward{j}{h}"):
            s2[j, half(h)] = both(behind, j, h).astype(BF16)
            push(s2.at[j, half(h)], r2.at[j, half(h)], S_R, RX + 16 + 2 * j + h, x_dev[-1])

    def onward(j, h):
        with mark(f"onward{j}{h}"):
            part = both(ahead, j, h)
            arrived(r0.at[j, half(h)], RX + 2 * j + h)
            s1[j, half(h)] = (part + r0[j, half(h)].astype(F32)).astype(BF16)
            push(s1.at[j, half(h)], r1.at[j, half(h)], S_R, RX + 8 + 2 * j + h, x_dev[1])

    def finish(j, h):
        with mark(f"finish{j}{h}"):
            part = both(0, j, h)
            arrived(r2.at[j, half(h)], RX + 16 + 2 * j + h)
            part = part + r2[j, half(h)].astype(F32)
            arrived(r1.at[j, half(h)], RX + 8 + 2 * j + h)
            fin[j, half(h)] = (part + r1[j, half(h)].astype(F32)).astype(BF16)
            d = order[j]
            rows = pl.ds(pl.multiple_of(zh * PART + h * HALF, 32), HALF)
            if d:
                push(fin.at[j, half(h)], res.at[rows, :], S_Z, RZ, at_zh(zhs(d)))
            elif h:
                fetch(fin.at[j], res.at[part_rows(zh), :])

    todo = (
        (2, 0), (1, 0), (3, 0), (2, 1), (1, 1), (3, 1), (2, 2), (1, 2), (3, 2), (0, 0), (2, 3), (1, 3), (3, 3), (0, 1), (0, 2), (0, 3),
    )
    then = {
        4: [(opposite, 0, 0), (opposite, 0, 1)],
        6: [(backward, 0, 0), (backward, 0, 1)],
        8: [(opposite, 1, 0)],
        9: [(backward, 1, 0)],
        11: [(onward, 0, 0), (onward, 0, 1)],
        12: [(opposite, 2, 0), (backward, 2, 0)],
        13: [(opposite, 1, 1), (backward, 1, 1)],
        15: [(onward, 1, 0), (opposite, 2, 1), (backward, 2, 1)],
    }
    for i, (offset, j) in enumerate(todo):
        with mark(f"second{i}"):
            if offset == 1:
                pair_product(j)
            elif offset != 3:
                second_product(offset, j)
        for step, at, h in then.get(i, ()):
            step(at, h)
    with mark("n2_0"):
        spread(norm2, S_N2, N2, 1, source_sums())
    finish(0, 0)
    finish(0, 1)
    onward(2, 0)
    onward(1, 1)
    opposite(3, 0)
    backward(3, 0)
    finish(1, 0)
    with mark("n2_1"):
        spread(norm2, S_N2, N2, 0, collect(norm2, N2, 1))
    onward(2, 1)
    opposite(3, 1)
    backward(3, 1)
    finish(2, 0)
    finish(1, 1)
    with mark("n2_2"):
        spread(norm2, S_N2, N2, 2, collect(norm2, N2, 0))
    onward(3, 0)
    finish(2, 1)
    onward(3, 1)
    finish(3, 0)
    finish(3, 1)
    with mark("n2_3"):
        sums[...] = collect(norm2, N2, 2) / TOKENS
        fetch(sums, src_out)
    with mark("zlast"):
        arrived(cr.at[0, pl.ds(0, 3)], RZ)
    with mark("drain"):
        local[-1].wait()
        local[-2].wait()
        drained(tok.at[pl.ds(0, 7), pl.ds(0, 256)], S_TZ)
        drained(tok.at[pl.ds(0, 12)], S_TY)
        drained(xb.at[pl.ds(0, 31)], S_X)
        for which in range(2):
            drained(act.at[which, pl.ds(0, 3)], S_A + which)
        drained(idb.at[pl.ds(0, 3)], S_I)
        drained(cr, S_CC)
        drained(cr.at[pl.ds(0, 3)], S_R)
        drained(cr.at[0, pl.ds(0, 3)], S_Z)
        for stage in range(3):
            drained(norm1.at[0, pl.ds(0, len(groups[stage]))], S_N1 + stage)
            drained(norm2.at[0, pl.ds(0, len(groups[stage]))], S_N2 + stage)


def emit(res, sums, out, src):
    for j in range(7):
        out[:, j * 128 : (j + 1) * 128] = res[j * 128 : (j + 1) * 128, :].T.astype(F32)
    src[...] = sums[0:1, :NSRC]


def body(tokens, gate_pre, up_act, hidden_cot, source_ids, data_weight, grad, moment_m, moment_v, val_adjoint):
    hbm = pl.BlockSpec(memory_space=pl.ANY)
    vmem = pl.BlockSpec(memory_space=pltpu.VMEM)
    turned, sums = pl.pallas_call(
        kernel,
        name="metagradient",
        out_shape=(jax.ShapeDtypeStruct((COLS, ROWS), BF16), jax.ShapeDtypeStruct((8, 128), F32)),
        in_specs=[hbm] * 10,
        out_specs=(hbm, hbm),
        scratch_shapes=[
            *[pltpu.VMEM((ROWS, COLS), F32)] * 4,
            *[pltpu.VMEM((ROWS, COLS), BF16)] * 3,
            pltpu.VMEM((16, TOK, 256), BF16),
            pltpu.VMEM((4, 512, ROWS), BF16),
            pltpu.VMEM((32, PART, 128), BF16),
            pltpu.VMEM((2, COLS, ROWS), BF16),
            pltpu.VMEM((2, 4, PART, ROWS), BF16),
            pltpu.VMEM((4, 8, ROWS), F32),
            pltpu.VMEM((3, 8, 8, 128), F32),
            pltpu.VMEM((3, 8, 8, 128), F32),
            pltpu.VMEM((PART, TOK), F32),
            pltpu.VMEM((PART, TOK), BF16),
            pltpu.VMEM((4, 4, 2, PART, 128), BF16),
            pltpu.VMEM((4, 4, PART, 128), BF16),
            *[pltpu.VMEM((4, PART, 128), BF16)] * 7,
            pltpu.VMEM((1, ROWS), jnp.int32),
            pltpu.SMEM((NSRC,), F32),
            pltpu.VMEM((8, 128), F32),
            pltpu.VMEM((128, TOK), F32),
            pltpu.SemaphoreType.DMA((16,)),
            pltpu.SemaphoreType.DMA((SEND.used,)),
            pltpu.SemaphoreType.DMA((RECV.used,)),
        ],
        compiler_params=pltpu.CompilerParams(
            collective_id=0, has_side_effects=True, vmem_limit_bytes=60 * 2**20
        ),
    )(
        tokens,
        gate_pre,
        up_act,
        hidden_cot,
        source_ids.reshape(1, ROWS),
        data_weight,
        grad,
        moment_m,
        moment_v,
        val_adjoint,
    )
    curvature, source_grad = pl.pallas_call(
        emit,
        name="emit",
        out_shape=(jax.ShapeDtypeStruct((ROWS, COLS), F32), jax.ShapeDtypeStruct((1, NSRC), F32)),
        grid=(2,),
        in_specs=[pl.BlockSpec((COLS // 2, ROWS), lambda i: (i, 0)), pl.BlockSpec((8, 128), lambda i: (0, 0))],
        out_specs=(pl.BlockSpec((ROWS, COLS // 2), lambda i: (0, i)), pl.BlockSpec((1, NSRC), lambda i: (0, 0))),
        compiler_params=pltpu.CompilerParams(vmem_limit_bytes=60 * 2**20),
    )(turned, sums)
    return curvature, source_grad.reshape(NSRC)


def solution(mesh):
    split = P("dp", "tensor")
    in_specs = (split, split, split, split, P("dp"), P(), split, split, split, split)
    return jax.shard_map(body, mesh=mesh, in_specs=in_specs, out_specs=(split, P()), check_vma=False)
```
